256 devices in a mesh: pts: 128 (over y, z, x), sta: 2 (over core).
Axes of the slice: x: 4, y: 4, z: 8, core: 2. Of those that a mesh axis runs over, the one named last changes fastest.
Arguments:
- greens: bfloat16 [2, 512, 262144], P(None, 'sta', 'pts'), may hold values from -6 to 6
- source: float32 [262144], P('pts'), may hold values from 0.2 to 5
- observed: float32 [2, 512, 512], P(None, None, 'sta'), may hold values from -12 to 12
- pair_mask: int32 [512, 512], P(None, 'sta'), may hold values 0 or 1
- block_ids: int32 [512], replicated, may hold values from 0 to 31
Outputs:
- kernel: float32 [262144], P('pts')
- adjoint: bfloat16 [2, 512, 512], P(None, None, 'sta')
The draws below stay inside these ranges and needn't reach their ends.
All inputs are finite; a program needn't handle non-finite values. No bound on the sum of `pair_mask` on one device may be relied on, other than what follows from the above.
Results may differ from the reference program's by a relative error of at most 0.0046.
Values may be sent and summed in bfloat16 or wider, within the bound.
A program may use at most 64 MiB of HBM per device.

```python
import math
import jax
import jax.numpy as jnp
from jax import lax

S = 512
PTS_DEV = 2048
NBLK = 32
X = 262144


def touch_ends(values, key, least, largest):
    longest = values.shape.index(max(values.shape))
    spots = []
    for shift in (0, 1):
        where = [jax.random.randint(jax.random.fold_in(key, axis), (), 0, length) for axis, length in enumerate(values.shape)]
        where[longest] = (where[longest] + shift) % values.shape[longest]
        spots.append(tuple(where))
    return values.at[spots[0]].set(least).at[spots[1]].set(largest)


def shard_levels(stream_key, dims, cuts, smallest, top_value):
    def one(position, shards_of):
        steps = jax.random.uniform(jax.random.fold_in(jax.random.fold_in(stream_key, 6), position), (shards_of,), jnp.float32, smallest / len(cuts), top_value / len(cuts))
        return jnp.repeat(jnp.exp(steps), dims[position] // shards_of).reshape((-1,) + (1,) * (len(dims) - position - 1))

    loudness = one(*cuts[0])
    for cut in cuts[1:]:
        loudness = loudness * one(*cut)
    return loudness


def scatter_about(rng, dims, scale, most, pieces=(), kind=jnp.bfloat16):
    drawn = jax.random.normal(rng, dims, jnp.float32) * scale
    if len(pieces) > 0:
        drawn = shard_levels(rng, dims, pieces, -0.22, 0.18) * drawn
    return jnp.clip(drawn, min=-most, max=most).astype(kind)


def setup_inputs(seed: int = 0) -> dict:
    seeds = jax.random.split(jax.random.key(seed), 6)
    return {
        "greens": scatter_about(seeds[0], (2, S, X), 1.0, 6.0, ((1, 2), (2, 128))),
        "source": jnp.clip(jnp.exp(math.log(5.0) - 3.218876 * jax.random.uniform(seeds[1], (X,), jnp.float32) ** shard_levels(seeds[1], (X,), ((0, 128),), -0.2, 0.2)), 0.2, 5.0),
        "observed": scatter_about(seeds[2], (2, S, S), 2.0, 12.0, ((2, 2),), jnp.float32),
        "pair_mask": touch_ends((jax.random.randint(seeds[3], (S, S), 0, 4) < 3).astype(jnp.int32), jax.random.fold_in(seeds[3], 1), 0, 1),
        "block_ids": touch_ends(jax.random.randint(seeds[4], (S,), 0, NBLK), jax.random.fold_in(seeds[4], 1), 0, NBLK - 1).astype(jnp.int32),
    }


def contract_last(left, right):
    return lax.dot_general(left, right, (((1,), (1,)), ((), ())), preferred_element_type=jnp.float32)


def contract_first(left, right):
    return lax.dot_general(left, right, (((0,), (0,)), ((), ())), preferred_element_type=jnp.float32)


def reference(greens, source, observed, pair_mask, block_ids):
    norm_factor = float(X) ** -0.5
    weighted = (source[None, None, :] * greens.astype(jnp.float32)).astype(jnp.bfloat16)
    corr_real = norm_factor * (contract_last(greens[0], weighted[0]) + contract_last(greens[1], weighted[1]))
    corr_imag = norm_factor * (contract_last(greens[1], weighted[0]) - contract_last(greens[0], weighted[1]))
    retained = ((pair_mask == 1) & (block_ids[:, None] != block_ids[None, :])).astype(jnp.float32)
    adj_real = (retained * (corr_real - observed[0])).astype(jnp.bfloat16)
    adj_imag = (retained * (corr_imag - observed[1])).astype(jnp.bfloat16)
    adjoint = jnp.stack([adj_real, adj_imag])

    def one_block(index):
        first_col = (index * PTS_DEV).astype(jnp.int32)
        block = lax.dynamic_slice_in_dim(greens, first_col, PTS_DEV, 2)
        wave_real = contract_first(adj_real, block[0]) + contract_first(adj_imag, block[1])
        wave_imag = contract_first(adj_real, block[1]) - contract_first(adj_imag, block[0])
        return norm_factor * jnp.sum(wave_real * block[0].astype(jnp.float32) + wave_imag * block[1].astype(jnp.float32), axis=0)

    kernel = lax.map(one_block, jnp.arange(X // PTS_DEV, dtype=jnp.int32)).reshape(X)
    return kernel, adjoint
```

```python
import functools

import jax
import jax.numpy as jnp
from jax import lax
from jax.experimental import pallas as pl
from jax.experimental.pallas import tpu as pltpu
from jax.sharding import PartitionSpec as P

NY, NZ, NX = 4, 8, 4
PLANE = NY * NX
HALF = 256
ROWS = 16
LANES = 128
MESH = pl.DeviceIdType.MESH


def dot_nt(left, right):
    return lax.dot_general(
        left, right, (((1,), (1,)), ((), ())), preferred_element_type=jnp.float32
    )


def dot_nn(left, right):
    return lax.dot_general(
        left, right, (((1,), (0,)), ((), ())), preferred_element_type=jnp.float32
    )


def kernel_body(
    norm_factor,
    greens_ref,
    source_ref,
    observed_ref,
    mask_ref,
    ids_ref,
    kernel_ref,
    adjoint_ref,
    g_all,
    weighted,
    part_buf,
    rs1_buf,
    rs2_send,
    rs2_buf,
    adj,
    adj_t,
    obs_buf,
    mask_buf,
    k_own,
    k_other,
    local_sem,
    gx_send,
    gx_recv,
    rs1_send_sem,
    rs1_recv_sem,
    rs2_send_sem,
    rs2_recv_sem,
    ag1_send_sem,
    ag1_recv_sem,
    ag2_send_sem,
    ag2_recv_sem,
    kx_send,
    kx_recv,
):
    points = greens_ref.shape[2]
    me = lax.axis_index("pts")
    c = lax.axis_index("sta")
    other = 1 - c
    x = me % NX
    z = (me // NX) % NZ
    y = me // (NX * NZ)
    k = y * NX + x

    def plane_peer(d):
        py = (y + d // NX) % NY
        px = (x + d % NX) % NX
        return py * NX + px, (py * NZ + z) * NX + px

    def line_peer(d):
        pz = (z + d) % NZ
        return pz, (y * NZ + pz) * NX + x

    part_z = z // 4
    step_z = (z // 2) % 2
    lanes_z = pl.multiple_of((z % 2) * LANES, LANES)
    half_z = (c + step_z) % 2
    row_k = pl.multiple_of(k * ROWS, ROWS)
    row_z = pl.multiple_of(half_z * HALF + k * ROWS, ROWS)

    load = pltpu.make_async_copy(greens_ref, g_all.at[c], local_sem.at[0])
    load.start()
    load_obs = pltpu.make_async_copy(
        observed_ref.at[part_z, pl.ds(row_z, ROWS), pl.ds(lanes_z, LANES)],
        obs_buf,
        local_sem.at[1],
    )
    load_obs.start()
    load_mask = pltpu.make_async_copy(
        mask_ref.at[pl.ds(row_z, ROWS), pl.ds(lanes_z, LANES)],
        mask_buf,
        local_sem.at[2],
    )
    load_mask.start()

    barrier = pltpu.get_barrier_semaphore()

    def greet_plane(d, carry):
        pl.semaphore_signal(
            barrier, inc=1, device_id=(plane_peer(d)[1], c), device_id_type=MESH
        )
        return carry

    def greet_line(d, carry):
        pl.semaphore_signal(
            barrier, inc=1, device_id=(line_peer(d)[1], c), device_id_type=MESH
        )
        return carry

    pl.semaphore_signal(barrier, inc=1, device_id=(me, other), device_id_type=MESH)
    lax.fori_loop(1, PLANE, greet_plane, 0)
    lax.fori_loop(1, NZ, greet_line, 0)
    pl.semaphore_wait(barrier, 1 + (PLANE - 1) + (NZ - 1))

    exchange = pltpu.make_async_remote_copy(
        src_ref=greens_ref,
        dst_ref=g_all.at[c],
        send_sem=gx_send,
        recv_sem=gx_recv,
        device_id=(me, other),
        device_id_type=MESH,
    )
    exchange.start()

    load.wait()
    source = source_ref[...]
    weighted[0] = (source * g_all[c, 0].astype(jnp.float32)).astype(jnp.bfloat16)
    weighted[1] = (source * g_all[c, 1].astype(jnp.float32)).astype(jnp.bfloat16)

    def rs1_copy(step, d):
        peer, peer_pts = plane_peer(d)
        return pltpu.make_async_remote_copy(
            src_ref=part_buf.at[step, peer],
            dst_ref=rs1_buf.at[step, d],
            send_sem=rs1_send_sem.at[step, d],
            recv_sem=rs1_recv_sem.at[step, d],
            device_id=(peer_pts, c),
            device_id_type=MESH,
        )

    def correlate(step):
        half = (c + step) % 2
        rows_re = g_all[half, 0]
        rows_im = g_all[half, 1]
        real = dot_nt(rows_re, weighted[0]) + dot_nt(rows_im, weighted[1])
        imag = dot_nt(rows_im, weighted[0]) - dot_nt(rows_re, weighted[1])
        shape = (PLANE, ROWS, HALF)
        part_buf[step, :, 0] = (norm_factor * real).astype(jnp.bfloat16).reshape(shape)
        part_buf[step, :, 1] = (norm_factor * imag).astype(jnp.bfloat16).reshape(shape)

        def send(d, carry):
            rs1_copy(step, d).start()
            return carry

        lax.fori_loop(1, PLANE, send, 0)

    correlate(0)
    exchange.wait_recv()
    correlate(1)

    for step in range(2):

        def add(d, total):
            rs1_copy(step, d).wait_recv()
            return total + rs1_buf[step, d].astype(jnp.float32)

        total = lax.fori_loop(1, PLANE, add, part_buf[step, k].astype(jnp.float32))
        for part in range(2):
            for lane in range(2):
                rs2_send[part * 4 + step * 2 + lane] = total[
                    part, :, lane * LANES : (lane + 1) * LANES
                ]

    def rs2_copy(d):
        peer, peer_pts = line_peer(d)
        return pltpu.make_async_remote_copy(
            src_ref=rs2_send.at[peer],
            dst_ref=rs2_buf.at[d],
            send_sem=rs2_send_sem.at[d],
            recv_sem=rs2_recv_sem.at[d],
            device_id=(peer_pts, c),
            device_id_type=MESH,
        )

    def rs2_start(d, carry):
        rs2_copy(d).start()
        return carry

    lax.fori_loop(1, NZ, rs2_start, 0)

    load_obs.wait()
    load_mask.wait()
    ids = ids_ref[...].astype(jnp.float32)
    stations = ids.shape[1]
    spot = lax.broadcasted_iota(jnp.int32, (ROWS, stations), 1)
    row = lax.broadcasted_iota(jnp.int32, (ROWS, stations), 0) + row_z
    row_ids = jnp.sum(jnp.where(spot == row, ids, 0.0), axis=1, keepdims=True)
    col_ids = ids_ref[:, pl.ds(pl.multiple_of(c * HALF + lanes_z, LANES), LANES)].astype(jnp.float32)
    keep = (mask_buf[...] == 1) & (row_ids != col_ids)
    retained = jnp.where(keep, 1.0, 0.0)

    def add_line(d, total):
        rs2_copy(d).wait_recv()
        return total + rs2_buf[d]

    corr = lax.fori_loop(1, NZ, add_line, rs2_send[z])
    block = adj.at[part_z, half_z, pl.ds(row_k, ROWS), pl.ds(lanes_z, LANES)]
    block[...] = (retained * (corr - obs_buf[...])).astype(jnp.bfloat16)

    def ag1_block(d):
        pz = (z - d + NZ) % NZ
        return adj.at[
            pz // 4,
            (c + (pz // 2) % 2) % 2,
            pl.ds(row_k, ROWS),
            pl.ds(pl.multiple_of((pz % 2) * LANES, LANES), LANES),
        ]

    def ag1_start(d, carry):
        pltpu.make_async_remote_copy(
            src_ref=block,
            dst_ref=block,
            send_sem=ag1_send_sem.at[d],
            recv_sem=ag1_recv_sem.at[d],
            device_id=(line_peer(d)[1], c),
            device_id_type=MESH,
        ).start()
        return carry

    def ag1_wait(d, carry):
        arrived = ag1_block(d)
        pltpu.make_async_remote_copy(
            src_ref=arrived,
            dst_ref=arrived,
            send_sem=ag1_send_sem.at[d],
            recv_sem=ag1_recv_sem.at[d],
            device_id=(line_peer(d)[1], c),
            device_id_type=MESH,
        ).wait_recv()
        return carry

    lax.fori_loop(1, NZ, ag1_start, 0)
    lax.fori_loop(1, NZ, ag1_wait, 0)

    def ag2_copy(rows, d):
        return pltpu.make_async_remote_copy(
            src_ref=adj.at[:, :, pl.ds(rows, ROWS), :],
            dst_ref=adj.at[:, :, pl.ds(rows, ROWS), :],
            send_sem=ag2_send_sem.at[d],
            recv_sem=ag2_recv_sem.at[d],
            device_id=(plane_peer(d)[1], c),
            device_id_type=MESH,
        )

    def ag2_start(d, carry):
        ag2_copy(row_k, d).start()
        return carry

    def ag2_wait(d, carry):
        from_y = (y - d // NX + NY) % NY
        from_x = (x - d % NX + NX) % NX
        rows = pl.multiple_of((from_y * NX + from_x) * ROWS, ROWS)
        ag2_copy(rows, d).wait_recv()
        return carry

    lax.fori_loop(1, PLANE, ag2_start, 0)
    lax.fori_loop(1, PLANE, ag2_wait, 0)

    store = pltpu.make_async_copy(adj, adjoint_ref, local_sem.at[3])
    store.start()

    for part in range(2):
        for half in range(2):
            adj_t[part, half] = adj[part, half].T

    width = 512

    @pl.loop(0, points // width)
    def wave(q):
        spots = pl.ds(pl.multiple_of(q * width, width), width)
        real = jnp.zeros((HALF, width), jnp.float32)
        imag = jnp.zeros((HALF, width), jnp.float32)
        for half in range(2):
            g_re = g_all[half, 0, :, spots]
            g_im = g_all[half, 1, :, spots]
            real += dot_nn(adj_t[0, half], g_re) + dot_nn(adj_t[1, half], g_im)
            imag += dot_nn(adj_t[0, half], g_im) - dot_nn(adj_t[1, half], g_re)
        own_re = g_all[c, 0, :, spots].astype(jnp.float32)
        own_im = g_all[c, 1, :, spots].astype(jnp.float32)
        k_own[:, spots] = norm_factor * jnp.sum(
            real * own_re + imag * own_im, axis=0, keepdims=True
        )

    swap = pltpu.make_async_remote_copy(
        src_ref=k_own,
        dst_ref=k_other,
        send_sem=kx_send,
        recv_sem=kx_recv,
        device_id=(me, other),
        device_id_type=MESH,
    )
    swap.start()

    exchange.wait_send()

    def sent_plane(d, carry):
        rs1_copy(0, d).wait_send()
        rs1_copy(1, d).wait_send()
        ag2_copy(row_k, d).wait_send()
        return carry

    def sent_line(d, carry):
        rs2_copy(d).wait_send()
        pltpu.make_async_remote_copy(
            src_ref=block,
            dst_ref=block,
            send_sem=ag1_send_sem.at[d],
            recv_sem=ag1_recv_sem.at[d],
            device_id=(line_peer(d)[1], c),
            device_id_type=MESH,
        ).wait_send()
        return carry

    lax.fori_loop(1, PLANE, sent_plane, 0)
    lax.fori_loop(1, NZ, sent_line, 0)
    swap.wait()
    kernel_ref[...] = k_own[...] + k_other[...]
    store.wait()


def body(greens, source, observed, pair_mask, block_ids):
    own_count, points = greens.shape[1], greens.shape[2]
    stations = observed.shape[1]
    norm_factor = float(points * lax.axis_size("pts")) ** (-0.5)
    vmem = pl.BlockSpec(memory_space=pltpu.VMEM)
    hbm = pl.BlockSpec(memory_space=pl.ANY)
    dma = pltpu.SemaphoreType.DMA
    bf16, f32 = jnp.bfloat16, jnp.float32
    flops = 2 * 2 * 4 * stations * own_count * points
    kernel, adjoint = pl.pallas_call(
        functools.partial(kernel_body, norm_factor),
        out_shape=(
            jax.ShapeDtypeStruct((1, points), f32),
            jax.ShapeDtypeStruct((2, 2, HALF, HALF), bf16),
        ),
        in_specs=[hbm, vmem, hbm, hbm, vmem],
        out_specs=(vmem, hbm),
        scratch_shapes=[
            pltpu.VMEM((2, 2, HALF, points), bf16),
            pltpu.VMEM((2, HALF, points), bf16),
            pltpu.VMEM((2, PLANE, 2, ROWS, HALF), bf16),
            pltpu.VMEM((2, PLANE, 2, ROWS, HALF), bf16),
            pltpu.VMEM((NZ, ROWS, LANES), f32),
            pltpu.VMEM((NZ, ROWS, LANES), f32),
            pltpu.VMEM((2, 2, HALF, HALF), bf16),
            pltpu.VMEM((2, 2, HALF, HALF), bf16),
            pltpu.VMEM((ROWS, LANES), f32),
            pltpu.VMEM((ROWS, LANES), jnp.int32),
            pltpu.VMEM((1, points), f32),
            pltpu.VMEM((1, points), f32),
            dma((4,)),
            dma,
            dma,
            dma((2, PLANE)),
            dma((2, PLANE)),
            dma((NZ,)),
            dma((NZ,)),
            dma((NZ,)),
            dma((NZ,)),
            dma((PLANE,)),
            dma((PLANE,)),
            dma,
            dma,
        ],
        compiler_params=pltpu.CompilerParams(
            collective_id=0, has_side_effects=True, vmem_limit_bytes=48 * 2**20
        ),
        cost_estimate=pl.CostEstimate(
            flops=flops, bytes_accessed=8 * 2**20, transcendentals=0
        ),
        name="noise_kernel",
    )(
        greens,
        source.reshape(1, points),
        observed,
        pair_mask,
        block_ids.reshape(1, stations),
    )
    return kernel.reshape(points), adjoint.reshape(2, stations, own_count)


def solution(mesh):
    placed = (P(None, "sta", "pts"), P("pts"), P(None, None, "sta"), P(None, "sta"), P())
    return jax.shard_map(
        body,
        mesh=mesh,
        in_specs=placed,
        out_specs=(P("pts"), P(None, None, "sta")),
        check_vma=False,
    )
```

```python
import functools

import jax
import jax.numpy as jnp
from jax import lax
from jax.experimental import pallas as pl
from jax.experimental.pallas import tpu as pltpu
from jax.sharding import PartitionSpec as P

NY, NZ, NX = 4, 8, 4
PLANE = NY * NX
HALF = 256
SUB = 128
ROWS = 16
GROUPS = SUB // ROWS
WIDTH = 512
CHUNKS = ((0, 0, 2), (1, 0, 1), (1, 1, 1))
MESH = pl.DeviceIdType.MESH


def dot_nt(left, right):
    return lax.dot_general(
        left, right, (((1,), (1,)), ((), ())), preferred_element_type=jnp.float32
    )


def dot_nn(left, right):
    return lax.dot_general(
        left, right, (((1,), (0,)), ((), ())), preferred_element_type=jnp.float32
    )


def kernel_body(
    norm_factor,
    greens_ref,
    source_hbm,
    observed_ref,
    mask_ref,
    ids_hbm,
    kernel_ref,
    adjoint_ref,
    g_all,
    weighted,
    adj,
    obs_buf,
    mask_buf,
    kept,
    source_ref,
    ids_ref,
    k_acc,
    k_own,
    k_other,
    local_sem,
    gx_send,
    gx_recv,
    rs_send,
    rs_recv,
    zx_send,
    zx_recv,
    ag_send,
    ag_recv,
    kx_send,
    kx_recv,
    *buffers,
):
    count = len(CHUNKS)
    part_bufs = buffers[:count]
    rs_bufs = buffers[count : 2 * count]
    zx_bufs = buffers[2 * count :]
    points = greens_ref.shape[2]
    me = lax.axis_index("pts")
    c = lax.axis_index("sta")
    other = 1 - c
    x = me % NX
    z = (me // NX) % NZ
    y = me // (NX * NZ)
    k = y * NX + x
    part_k = k // GROUPS
    row_k = pl.multiple_of((k % GROUPS) * ROWS, ROWS)

    def plane_peer(d):
        py = (y + d // NX) % NY
        px = (x + d % NX) % NX
        return py * NX + px, (py * NZ + z) * NX + px

    def line_peer(d):
        pz = (z + d) % NZ
        return pz, (y * NZ + pz) * NX + x

    def each(start, stop, step):
        def once(d, carry):
            step(d)
            return carry

        lax.fori_loop(start, stop, once, 0)

    load = pltpu.make_async_copy(greens_ref, g_all.at[c], local_sem.at[0])
    load.start()
    load_source = pltpu.make_async_copy(source_hbm, source_ref, local_sem.at[1])
    load_source.start()

    barrier = pltpu.get_barrier_semaphore()

    def greet(pts, sta):
        pl.semaphore_signal(barrier, inc=1, device_id=(pts, sta), device_id_type=MESH)

    greet(me, other)
    each(1, PLANE, lambda d: greet(plane_peer(d)[1], c))
    each(1, NZ, lambda d: greet(line_peer(d)[1], c))
    pl.semaphore_wait(barrier, 1 + (PLANE - 1) + (NZ - 1))

    def exchange(sub):
        rows = pl.ds(sub * SUB, SUB)
        return pltpu.make_async_remote_copy(
            src_ref=greens_ref.at[:, rows, :],
            dst_ref=g_all.at[c, :, rows, :],
            send_sem=gx_send.at[sub],
            recv_sem=gx_recv.at[sub],
            device_id=(me, other),
            device_id_type=MESH,
        )

    for sub in range(2):
        exchange(sub).start()

    load_ids = pltpu.make_async_copy(ids_hbm, ids_ref, local_sem.at[2])
    load_ids.start()
    load_obs = pltpu.make_async_copy(
        observed_ref.at[part_k, :, :, pl.ds(row_k, ROWS), :], obs_buf, local_sem.at[3]
    )
    load_obs.start()
    load_mask = pltpu.make_async_copy(
        mask_ref.at[:, :, pl.ds(row_k, ROWS), :], mask_buf, local_sem.at[4]
    )
    load_mask.start()

    load_source.wait()
    load.wait()
    source = source_ref[...]
    weighted[0] = (source * g_all[c, 0].astype(jnp.float32)).astype(jnp.bfloat16)
    weighted[1] = (source * g_all[c, 1].astype(jnp.float32)).astype(jnp.bfloat16)

    def rs_copy(chunk, d):
        peer, peer_pts = plane_peer(d)
        return pltpu.make_async_remote_copy(
            src_ref=part_bufs[chunk].at[peer],
            dst_ref=rs_bufs[chunk].at[d],
            send_sem=rs_send.at[chunk, d],
            recv_sem=rs_recv.at[chunk, d],
            device_id=(peer_pts, c),
            device_id_type=MESH,
        )

    def zx_copy(chunk, d, slot):
        return pltpu.make_async_remote_copy(
            src_ref=zx_bufs[chunk].at[slot],
            dst_ref=zx_bufs[chunk].at[slot],
            send_sem=zx_send.at[chunk, d],
            recv_sem=zx_recv.at[chunk, d],
            device_id=(line_peer(d)[1], c),
            device_id_type=MESH,
        )

    def half_of(chunk):
        return (c + CHUNKS[chunk][0]) % 2

    def ag_copy(chunk, d, owner):
        _, first, subs = CHUNKS[chunk]
        rows = pl.multiple_of((owner % GROUPS) * ROWS, ROWS)
        block = adj.at[
            owner // GROUPS, half_of(chunk), pl.ds(first, subs), pl.ds(rows, ROWS), :
        ]
        return pltpu.make_async_remote_copy(
            src_ref=block,
            dst_ref=block,
            send_sem=ag_send.at[chunk, d],
            recv_sem=ag_recv.at[chunk, d],
            device_id=(plane_peer(d)[1], c),
            device_id_type=MESH,
        )

    def correlate(chunk):
        _, first, subs = CHUNKS[chunk]
        rows = pl.ds(first * SUB, subs * SUB)
        rows_re = g_all[half_of(chunk), 0, rows, :]
        rows_im = g_all[half_of(chunk), 1, rows, :]
        real = dot_nt(rows_re, weighted[0]) + dot_nt(rows_im, weighted[1])
        imag = dot_nt(rows_im, weighted[0]) - dot_nt(rows_re, weighted[1])
        for part, value in enumerate((real, imag)):
            for sub in range(subs):
                block = value[sub * SUB : (sub + 1) * SUB].astype(jnp.bfloat16)
                part_bufs[chunk][part * GROUPS : (part + 1) * GROUPS, sub] = block.reshape(
                    GROUPS, ROWS, HALF
                )
        each(1, PLANE, lambda d: rs_copy(chunk, d).start())

    def reduce_plane(chunk):
        def add(d, total):
            rs_copy(chunk, d).wait_recv()
            return total + rs_bufs[chunk][d].astype(jnp.float32)

        total = lax.fori_loop(1, PLANE, add, part_bufs[chunk][k].astype(jnp.float32))
        zx_bufs[chunk][z] = total.astype(jnp.bfloat16)
        each(1, NZ, lambda d: zx_copy(chunk, d, z).start())

    def make_adjoint(chunk):
        _, first, subs = CHUNKS[chunk]
        each(1, NZ, lambda d: zx_copy(chunk, d, (z - d + NZ) % NZ).wait_recv())
        half = half_of(chunk)
        corr = zx_bufs[chunk][0].astype(jnp.float32)
        for slot in range(1, NZ):
            corr = corr + zx_bufs[chunk][slot].astype(jnp.float32)
        for sub in range(subs):
            value = kept[half, first + sub] * (
                norm_factor * corr[sub] - obs_buf[half, first + sub]
            )
            adj[part_k, half, first + sub, pl.ds(row_k, ROWS), :] = value.astype(
                jnp.bfloat16
            )
        each(1, PLANE, lambda d: ag_copy(chunk, d, k).start())

    def gather(chunk):
        def wait(d):
            from_y = (y - d // NX + NY) % NY
            from_x = (x - d % NX + NX) % NX
            ag_copy(chunk, d, from_y * NX + from_x).wait_recv()

        each(1, PLANE, wait)

    def store(chunk):
        _, first, subs = CHUNKS[chunk]
        half = half_of(chunk)
        return pltpu.make_async_copy(
            adj.at[:, half, pl.ds(first, subs)],
            adjoint_ref.at[:, half, pl.ds(first, subs)],
            local_sem.at[5 + chunk],
        )

    def swap(piece):
        spots = pl.ds(piece * WIDTH, WIDTH)
        return pltpu.make_async_remote_copy(
            src_ref=k_own.at[:, spots],
            dst_ref=k_other.at[:, spots],
            send_sem=kx_send.at[piece],
            recv_sem=kx_recv.at[piece],
            device_id=(me, other),
            device_id_type=MESH,
        )

    def wave(chunk):
        _, first, subs = CHUNKS[chunk]
        half = half_of(chunk)
        count_rows = subs * SUB
        rows = pl.ds(first * SUB, count_rows)
        res_re = adj[0, half, first : first + subs].reshape(count_rows, HALF)
        res_im = adj[1, half, first : first + subs].reshape(count_rows, HALF)
        for piece in range(points // WIDTH):
            spots = pl.ds(piece * WIDTH, WIDTH)
            own_re = g_all[c, 0, :, spots]
            own_im = g_all[c, 1, :, spots]
            real = dot_nn(res_re, own_re) - dot_nn(res_im, own_im)
            imag = dot_nn(res_re, own_im) + dot_nn(res_im, own_re)
            row_re = g_all[half, 0, rows, spots].astype(jnp.float32)
            row_im = g_all[half, 1, rows, spots].astype(jnp.float32)
            terms = real * row_re + imag * row_im
            terms = jnp.sum(terms.reshape(count_rows // 8, 8, WIDTH), axis=0)
            if chunk > 0:
                terms = terms + k_acc[:, spots]
            if chunk < count - 1:
                k_acc[:, spots] = terms
            else:
                k_own[:, spots] = norm_factor * jnp.sum(terms, axis=0, keepdims=True)
                swap(piece).start()

    correlate(0)
    for chunk in range(1, count):
        exchange(CHUNKS[chunk][1]).wait_recv()
        correlate(chunk)

    load_ids.wait()
    load_mask.wait()
    load_obs.wait()
    ids = ids_ref[...].astype(jnp.float32)
    stations = ids.shape[1]
    col_ids = ids_ref[:, pl.ds(pl.multiple_of(c * HALF, HALF), HALF)].astype(jnp.float32)
    spot = lax.broadcasted_iota(jnp.int32, (ROWS, stations), 1)
    row = lax.broadcasted_iota(jnp.int32, (ROWS, stations), 0) + row_k
    for half in range(2):
        for sub in range(2):
            here = spot == row + (half * HALF + sub * SUB)
            row_ids = jnp.sum(jnp.where(here, ids, 0.0), axis=1, keepdims=True)
            keep = (mask_buf[half, sub] == 1) & (row_ids != col_ids)
            kept[half, sub] = jnp.where(keep, 1.0, 0.0)

    for chunk in range(count):
        reduce_plane(chunk)
    for sub in range(2):
        exchange(sub).wait_send()
    for chunk in range(count):
        make_adjoint(chunk)
    for chunk in range(count):
        each(1, PLANE, lambda d: rs_copy(chunk, d).wait_send())
        each(1, NZ, lambda d: zx_copy(chunk, d, z).wait_send())
    for chunk in range(count):
        gather(chunk)
        store(chunk).start()
        wave(chunk)

    for chunk in range(count):
        each(1, PLANE, lambda d: ag_copy(chunk, d, k).wait_send())
        store(chunk).wait()
    for piece in range(points // WIDTH):
        swap(piece).wait()
    kernel_ref[...] = k_own[...] + k_other[...]


def body(greens, source, observed, pair_mask, block_ids):
    own_count, points = greens.shape[1], greens.shape[2]
    stations = observed.shape[1]
    norm_factor = float(points * lax.axis_size("pts")) ** (-0.5)
    vmem = pl.BlockSpec(memory_space=pltpu.VMEM)
    hbm = pl.BlockSpec(memory_space=pltpu.HBM)
    anywhere = pl.BlockSpec(memory_space=pl.ANY)
    dma = pltpu.SemaphoreType.DMA
    bf16, f32 = jnp.bfloat16, jnp.float32
    count = len(CHUNKS)
    pieces = points // WIDTH

    def blocks(slots):
        return [pltpu.VMEM((slots, subs, ROWS, HALF), bf16) for _, _, subs in CHUNKS]

    operands = (
        greens,
        source.reshape(1, points),
        observed.reshape(2, 2, 2, SUB, HALF),
        pair_mask.reshape(2, 2, SUB, HALF),
        block_ids.reshape(1, stations),
    )
    kernel, adjoint = pl.pallas_call(
        functools.partial(kernel_body, norm_factor),
        out_shape=(
            jax.ShapeDtypeStruct((1, points), f32),
            jax.ShapeDtypeStruct((2, 2, 2, SUB, HALF), bf16),
        ),
        in_specs=[hbm] * 5,
        out_specs=(vmem, anywhere),
        scratch_shapes=[
            pltpu.VMEM((2, 2, HALF, points), bf16),
            pltpu.VMEM((2, HALF, points), bf16),
            pltpu.VMEM((2, 2, 2, SUB, HALF), bf16),
            pltpu.VMEM((2, 2, ROWS, HALF), f32),
            pltpu.VMEM((2, 2, ROWS, HALF), jnp.int32),
            pltpu.VMEM((2, 2, ROWS, HALF), f32),
            pltpu.VMEM((1, points), f32),
            pltpu.VMEM((1, stations), jnp.int32),
            pltpu.VMEM((8, points), f32),
            pltpu.VMEM((1, points), f32),
            pltpu.VMEM((1, points), f32),
            dma((5 + count,)),
            dma((2,)),
            dma((2,)),
            dma((count, PLANE)),
            dma((count, PLANE)),
            dma((count, NZ)),
            dma((count, NZ)),
            dma((count, PLANE)),
            dma((count, PLANE)),
            dma((pieces,)),
            dma((pieces,)),
            *blocks(PLANE),
            *blocks(PLANE),
            *blocks(NZ),
        ],
        compiler_params=pltpu.CompilerParams(
            collective_id=0, has_side_effects=True, vmem_limit_bytes=48 * 2**20
        ),
        cost_estimate=pl.CostEstimate(
            flops=16 * stations * own_count * points,
            bytes_accessed=8 * 2**20,
            transcendentals=0,
        ),
        name="noise_kernel",
    )(*(pltpu.with_memory_space_constraint(operand, pltpu.HBM) for operand in operands))
    return kernel.reshape(points), adjoint.reshape(2, stations, own_count)


def solution(mesh):
    placed = (P(None, "sta", "pts"), P("pts"), P(None, None, "sta"), P(None, "sta"), P())
    return jax.shard_map(
        body,
        mesh=mesh,
        in_specs=placed,
        out_specs=(P("pts"), P(None, None, "sta")),
        check_vma=False,
    )
```

```python
import functools

import jax
import jax.numpy as jnp
from jax import lax
from jax.experimental import pallas as pl
from jax.experimental.pallas import tpu as pltpu
from jax.sharding import PartitionSpec as P

NY, NZ, NX = 4, 8, 4
PLANE = NY * NX
HALF = 256
SUB = 128
ROWS = 16
GROUPS = SUB // ROWS
WIDTH = 512
CHUNKS = ((0, 0, 2), (1, 0, 2))
PIECES = 4
MESH = pl.DeviceIdType.MESH
PLANE_PEERS = (
    (2, 2), (3, 2), (2, 3), (1, 2), (2, 1), (0, 2), (2, 0), (3, 1),
    (1, 3), (3, 3), (1, 1), (3, 0), (0, 3), (1, 0), (0, 1),
)
LINE_PEERS = (4, 3, 5, 2, 6, 1, 7)


def dot_nt(left, right):
    return lax.dot_general(
        left, right, (((1,), (1,)), ((), ())), preferred_element_type=jnp.float32
    )


def dot_nn(left, right):
    return lax.dot_general(
        left, right, (((1,), (0,)), ((), ())), preferred_element_type=jnp.float32
    )


def kernel_body(
    norm_factor,
    greens_ref,
    source_hbm,
    observed_ref,
    mask_ref,
    ids_hbm,
    kernel_ref,
    adjoint_ref,
    g_all,
    weighted,
    adj,
    obs_buf,
    mask_buf,
    kept,
    source_ref,
    ids_ref,
    k_acc,
    k_own,
    k_other,
    known,
    local_sem,
    gx_send,
    gx_recv,
    rs_send,
    rs_recv,
    zx_send,
    zx_recv,
    ag_send,
    ag_recv,
    kx_send,
    kx_recv,
    *buffers,
):
    count = len(CHUNKS)
    part_bufs = buffers[:count]
    rs_bufs = buffers[count : 2 * count]
    zx_bufs = buffers[2 * count :]
    points = greens_ref.shape[2]
    me = lax.axis_index("pts")
    c = lax.axis_index("sta")
    other = 1 - c
    x = me % NX
    z = (me // NX) % NZ
    y = me // (NX * NZ)
    k = y * NX + x
    part_k = k // GROUPS
    row_k = pl.multiple_of((k % GROUPS) * ROWS, ROWS)

    def plane_peer(d):
        py = (y + d // NX) % NY
        px = (x + d % NX) % NX
        return py * NX + px, (py * NZ + z) * NX + px

    def line_peer(d):
        pz = (z + d) % NZ
        return pz, (y * NZ + pz) * NX + x

    def each(start, stop, step):
        def once(d, carry):
            step(d)
            return carry

        lax.fori_loop(start, stop, once, 0)

    load = pltpu.make_async_copy(greens_ref, g_all.at[c], local_sem.at[0])
    load.start()
    load_source = pltpu.make_async_copy(source_hbm, source_ref, local_sem.at[1])
    load_source.start()

    barrier = pltpu.get_barrier_semaphore()
    ring = [plane_peer(d)[1] for d in range(1, NX)]
    column = [plane_peer(d * NX)[1] for d in range(1, NY)]
    beside = [line_peer(d)[1] for d in (1, NZ - 1)]
    beyond = [line_peer(d)[1] for d in (2, NZ - 2)]
    pl.semaphore_signal(barrier, inc=1, device_id=(me, other), device_id_type=MESH)
    for pts in (*ring, *column, *beyond, *beside):
        pl.semaphore_signal(barrier, inc=1, device_id=(pts, c), device_id_type=MESH)

    def exchange(piece):
        span = points // PIECES
        spots = pl.ds(piece * span, span)
        return pltpu.make_async_remote_copy(
            src_ref=g_all.at[c, :, :, spots],
            dst_ref=g_all.at[c, :, :, spots],
            send_sem=gx_send.at[piece],
            recv_sem=gx_recv.at[piece],
            device_id=(me, other),
            device_id_type=MESH,
        )

    load_ids = pltpu.make_async_copy(ids_hbm, ids_ref, local_sem.at[2])
    load_ids.start()
    load_obs = pltpu.make_async_copy(
        observed_ref.at[part_k, :, :, pl.ds(row_k, ROWS), :], obs_buf, local_sem.at[3]
    )
    load_obs.start()
    load_mask = pltpu.make_async_copy(
        mask_ref.at[:, :, pl.ds(row_k, ROWS), :], mask_buf, local_sem.at[4]
    )
    load_mask.start()

    load_source.wait()
    load.wait()
    source = source_ref[...]
    weighted[0] = (source * g_all[c, 0].astype(jnp.float32)).astype(jnp.bfloat16)
    weighted[1] = (source * g_all[c, 1].astype(jnp.float32)).astype(jnp.bfloat16)

    def rs_copy(chunk, d):
        peer, peer_pts = plane_peer(d)
        return pltpu.make_async_remote_copy(
            src_ref=part_bufs[chunk].at[peer],
            dst_ref=rs_bufs[chunk].at[d],
            send_sem=rs_send.at[chunk, d],
            recv_sem=rs_recv.at[chunk, d],
            device_id=(peer_pts, c),
            device_id_type=MESH,
        )

    def zx_copy(chunk, d, slot):
        return pltpu.make_async_remote_copy(
            src_ref=zx_bufs[chunk].at[slot],
            dst_ref=zx_bufs[chunk].at[slot],
            send_sem=zx_send.at[chunk, d],
            recv_sem=zx_recv.at[chunk, d],
            device_id=(line_peer(d)[1], c),
            device_id_type=MESH,
        )

    def half_of(chunk):
        return (c + CHUNKS[chunk][0]) % 2

    def ag_copy(chunk, d, owner):
        _, first, subs = CHUNKS[chunk]
        rows = pl.multiple_of((owner % GROUPS) * ROWS, ROWS)
        block = adj.at[
            owner // GROUPS, half_of(chunk), pl.ds(first, subs), pl.ds(rows, ROWS), :
        ]
        return pltpu.make_async_remote_copy(
            src_ref=block,
            dst_ref=block,
            send_sem=ag_send.at[chunk, d],
            recv_sem=ag_recv.at[chunk, d],
            device_id=(plane_peer(d)[1], c),
            device_id_type=MESH,
        )

    def correlate(chunk):
        half = half_of(chunk)
        real = jnp.zeros((HALF, HALF), jnp.float32)
        imag = jnp.zeros((HALF, HALF), jnp.float32)
        span = points // PIECES
        for piece in range(PIECES):
            if chunk > 0:
                exchange(piece).wait_recv()
            spots = pl.ds(piece * span, span)
            rows_re = g_all[half, 0, :, spots]
            rows_im = g_all[half, 1, :, spots]
            own_re = weighted[0, :, spots]
            own_im = weighted[1, :, spots]
            real += dot_nt(rows_re, own_re) + dot_nt(rows_im, own_im)
            imag += dot_nt(rows_im, own_re) - dot_nt(rows_re, own_im)
        for part, value in enumerate((real, imag)):
            for sub in range(2):
                block = value[sub * SUB : (sub + 1) * SUB].astype(jnp.bfloat16)
                part_bufs[chunk][part * GROUPS : (part + 1) * GROUPS, sub] = block.reshape(
                    GROUPS, ROWS, HALF
                )

    def scatter(chunk, peers=PLANE_PEERS):
        for dy, dx in peers:
            rs_copy(chunk, dy * NX + dx).start()

    def reduce_plane(chunk):
        def add(d, total):
            rs_copy(chunk, d).wait_recv()
            return total + rs_bufs[chunk][d].astype(jnp.float32)

        total = lax.fori_loop(1, PLANE, add, part_bufs[chunk][k].astype(jnp.float32))
        zx_bufs[chunk][z] = total.astype(jnp.bfloat16)
        for d in LINE_PEERS:
            zx_copy(chunk, d, z).start()

    def make_adjoint(chunk):
        _, first, subs = CHUNKS[chunk]
        each(1, NZ, lambda d: zx_copy(chunk, d, (z - d + NZ) % NZ).wait_recv())
        half = half_of(chunk)
        corr = zx_bufs[chunk][0].astype(jnp.float32)
        for slot in range(1, NZ):
            corr = corr + zx_bufs[chunk][slot].astype(jnp.float32)
        for sub in range(subs):
            value = kept[half, first + sub] * (
                norm_factor * corr[sub] - obs_buf[half, first + sub]
            )
            adj[part_k, half, first + sub, pl.ds(row_k, ROWS), :] = value.astype(
                jnp.bfloat16
            )
        for dy, dx in PLANE_PEERS:
            ag_copy(chunk, dy * NX + dx, k).start()

    def gather(chunk):
        def wait(d):
            from_y = (y - d // NX + NY) % NY
            from_x = (x - d % NX + NX) % NX
            ag_copy(chunk, d, from_y * NX + from_x).wait_recv()

        each(1, PLANE, wait)

    def store(chunk):
        _, first, subs = CHUNKS[chunk]
        half = half_of(chunk)
        return pltpu.make_async_copy(
            adj.at[:, half, pl.ds(first, subs)],
            adjoint_ref.at[:, half, pl.ds(first, subs)],
            local_sem.at[5 + chunk],
        )

    def swap(piece):
        spots = pl.ds(piece * WIDTH, WIDTH)
        return pltpu.make_async_remote_copy(
            src_ref=k_own.at[:, spots],
            dst_ref=k_other.at[:, spots],
            send_sem=kx_send.at[piece],
            recv_sem=kx_recv.at[piece],
            device_id=(me, other),
            device_id_type=MESH,
        )

    def wave(chunk):
        _, first, subs = CHUNKS[chunk]
        half = half_of(chunk)
        count_rows = subs * SUB
        rows = pl.ds(first * SUB, count_rows)
        res_re = adj[0, half, first : first + subs].reshape(count_rows, HALF)
        res_im = adj[1, half, first : first + subs].reshape(count_rows, HALF)
        for piece in range(points // WIDTH):
            spots = pl.ds(piece * WIDTH, WIDTH)
            own_re = g_all[c, 0, :, spots]
            own_im = g_all[c, 1, :, spots]
            real = dot_nn(res_re, own_re) - dot_nn(res_im, own_im)
            imag = dot_nn(res_re, own_im) + dot_nn(res_im, own_re)
            row_re = g_all[half, 0, rows, spots].astype(jnp.float32)
            row_im = g_all[half, 1, rows, spots].astype(jnp.float32)
            terms = real * row_re + imag * row_im
            terms = jnp.sum(terms.reshape(count_rows // 8, 8, WIDTH), axis=0)
            if chunk > 0:
                terms = terms + k_acc[:, spots]
            if chunk < count - 1:
                k_acc[:, spots] = terms
            else:
                k_own[:, spots] = norm_factor * jnp.sum(terms, axis=0, keepdims=True)
                swap(piece).start()

    correlate(0)
    pl.semaphore_wait(barrier, 1 + len(ring) + len(column) + len(beside) + len(beyond))
    for piece in range(PIECES):
        exchange(piece).start()
    for pts in (*ring, *beyond):
        pl.semaphore_signal(known, inc=1, device_id=(pts, c), device_id_type=MESH)
    scatter(0, [(dy, dx) for dy, dx in PLANE_PEERS if dy * dx == 0])

    load_ids.wait()
    load_mask.wait()
    load_obs.wait()
    ids = ids_ref[...].astype(jnp.float32)
    stations = ids.shape[1]
    col_ids = ids_ref[:, pl.ds(pl.multiple_of(c * HALF, HALF), HALF)].astype(jnp.float32)
    spot = lax.broadcasted_iota(jnp.int32, (ROWS, stations), 1)
    row = lax.broadcasted_iota(jnp.int32, (ROWS, stations), 0) + row_k
    for half in range(2):
        for sub in range(2):
            here = spot == row + (half * HALF + sub * SUB)
            row_ids = jnp.sum(jnp.where(here, ids, 0.0), axis=1, keepdims=True)
            keep = (mask_buf[half, sub] == 1) & (row_ids != col_ids)
            kept[half, sub] = jnp.where(keep, 1.0, 0.0)

    pl.semaphore_wait(known, len(ring) + len(beyond))
    scatter(0, [(dy, dx) for dy, dx in PLANE_PEERS if dy * dx != 0])
    for chunk in range(1, count):
        correlate(chunk)
        scatter(chunk)
    for chunk in range(count):
        reduce_plane(chunk)
    for piece in range(PIECES):
        exchange(piece).wait_send()
    for chunk in range(count):
        each(1, PLANE, lambda d: rs_copy(chunk, d).wait_send())
    for chunk in range(count):
        make_adjoint(chunk)
    for chunk in range(count):
        each(1, NZ, lambda d: zx_copy(chunk, d, z).wait_send())
    for chunk in range(count):
        if chunk == count - 1:
            for sent in range(count - 1):
                each(1, PLANE, lambda d: ag_copy(sent, d, k).wait_send())
        gather(chunk)
        store(chunk).start()
        wave(chunk)

    each(1, PLANE, lambda d: ag_copy(count - 1, d, k).wait_send())
    for chunk in range(count):
        store(chunk).wait()
    for piece in range(points // WIDTH):
        swap(piece).wait()
    kernel_ref[...] = k_own[...] + k_other[...]


def body(greens, source, observed, pair_mask, block_ids):
    own_count, points = greens.shape[1], greens.shape[2]
    stations = observed.shape[1]
    norm_factor = float(points * lax.axis_size("pts")) ** (-0.5)
    vmem = pl.BlockSpec(memory_space=pltpu.VMEM)
    hbm = pl.BlockSpec(memory_space=pltpu.HBM)
    anywhere = pl.BlockSpec(memory_space=pl.ANY)
    dma = pltpu.SemaphoreType.DMA
    bf16, f32 = jnp.bfloat16, jnp.float32
    count = len(CHUNKS)
    pieces = points // WIDTH

    def blocks(slots):
        return [pltpu.VMEM((slots, subs, ROWS, HALF), bf16) for _, _, subs in CHUNKS]

    operands = (
        greens,
        source.reshape(1, points),
        observed.reshape(2, 2, 2, SUB, HALF),
        pair_mask.reshape(2, 2, SUB, HALF),
        block_ids.reshape(1, stations),
    )
    kernel, adjoint = pl.pallas_call(
        functools.partial(kernel_body, norm_factor),
        out_shape=(
            jax.ShapeDtypeStruct((1, points), f32),
            jax.ShapeDtypeStruct((2, 2, 2, SUB, HALF), bf16),
        ),
        in_specs=[hbm] * 5,
        out_specs=(vmem, anywhere),
        scratch_shapes=[
            pltpu.VMEM((2, 2, HALF, points), bf16),
            pltpu.VMEM((2, HALF, points), bf16),
            pltpu.VMEM((2, 2, 2, SUB, HALF), bf16),
            pltpu.VMEM((2, 2, ROWS, HALF), f32),
            pltpu.VMEM((2, 2, ROWS, HALF), jnp.int32),
            pltpu.VMEM((2, 2, ROWS, HALF), f32),
            pltpu.VMEM((1, points), f32),
            pltpu.VMEM((1, stations), jnp.int32),
            pltpu.VMEM((8, points), f32),
            pltpu.VMEM((1, points), f32),
            pltpu.VMEM((1, points), f32),
            pltpu.SemaphoreType.REGULAR,
            dma((5 + count,)),
            dma((PIECES,)),
            dma((PIECES,)),
            dma((count, PLANE)),
            dma((count, PLANE)),
            dma((count, NZ)),
            dma((count, NZ)),
            dma((count, PLANE)),
            dma((count, PLANE)),
            dma((pieces,)),
            dma((pieces,)),
            *blocks(PLANE),
            *blocks(PLANE),
            *blocks(NZ),
        ],
        compiler_params=pltpu.CompilerParams(
            collective_id=0, has_side_effects=True, vmem_limit_bytes=48 * 2**20
        ),
        cost_estimate=pl.CostEstimate(
            flops=16 * stations * own_count * points,
            bytes_accessed=8 * 2**20,
            transcendentals=0,
        ),
        name="noise_kernel",
    )(*(pltpu.with_memory_space_constraint(operand, pltpu.HBM) for operand in operands))
    return kernel.reshape(points), adjoint.reshape(2, stations, own_count)


def solution(mesh):
    placed = (P(None, "sta", "pts"), P("pts"), P(None, None, "sta"), P(None, "sta"), P())
    return jax.shard_map(
        body,
        mesh=mesh,
        in_specs=placed,
        out_specs=(P("pts"), P(None, None, "sta")),
        check_vma=False,
    )
```

```python
import functools

import jax
import jax.numpy as jnp
from jax import lax
from jax.experimental import pallas as pl
from jax.experimental.pallas import tpu as pltpu
from jax.sharding import PartitionSpec as P

NY, NZ, NX = 4, 8, 4
PLANE = NY * NX
HALF = 256
SUB = 128
ROWS = 16
GROUPS = SUB // ROWS
WIDTH = 512
CHUNKS = ((0, 0, 2), (1, 0, 2))
PIECES = 4
MESH = pl.DeviceIdType.MESH
PLANE_PEERS = (
    (2, 2), (3, 2), (2, 3), (1, 2), (2, 1), (0, 2), (2, 0), (3, 1),
    (1, 3), (3, 3), (1, 1), (3, 0), (0, 3), (1, 0), (0, 1),
)
LINE_PEERS = (4, 3, 5, 2, 6, 1, 7)


def dot_nt(left, right):
    return lax.dot_general(
        left, right, (((1,), (1,)), ((), ())), preferred_element_type=jnp.float32
    )


def dot_nn(left, right):
    return lax.dot_general(
        left, right, (((1,), (0,)), ((), ())), preferred_element_type=jnp.float32
    )


def kernel_body(
    norm_factor,
    greens_ref,
    source_hbm,
    observed_ref,
    mask_ref,
    ids_hbm,
    kernel_ref,
    adjoint_ref,
    g_all,
    weighted,
    adj,
    obs_buf,
    mask_buf,
    kept,
    source_ref,
    ids_ref,
    k_acc,
    k_own,
    k_other,
    known,
    load_sem,
    local_sem,
    gx_send,
    gx_recv,
    rs_send,
    rs_recv,
    zx_send,
    zx_recv,
    ag_send,
    ag_recv,
    kx_send,
    kx_recv,
    *buffers,
):
    count = len(CHUNKS)
    part_bufs = buffers[:count]
    rs_bufs = buffers[count : 2 * count]
    zx_bufs = buffers[2 * count :]
    points = greens_ref.shape[2]
    me = lax.axis_index("pts")
    c = lax.axis_index("sta")
    other = 1 - c
    x = me % NX
    z = (me // NX) % NZ
    y = me // (NX * NZ)
    k = y * NX + x
    part_k = k // GROUPS
    row_k = pl.multiple_of((k % GROUPS) * ROWS, ROWS)

    def plane_peer(d):
        py = (y + d // NX) % NY
        px = (x + d % NX) % NX
        return py * NX + px, (py * NZ + z) * NX + px

    def line_peer(d):
        pz = (z + d) % NZ
        return pz, (y * NZ + pz) * NX + x

    def each(start, stop, step):
        def once(d, carry):
            step(d)
            return carry

        lax.fori_loop(start, stop, once, 0)

    barrier = pltpu.get_barrier_semaphore()
    ring = [plane_peer(d)[1] for d in range(1, NX)]
    column = [plane_peer(d * NX)[1] for d in range(1, NY)]
    beside = [line_peer(d)[1] for d in (1, NZ - 1)]
    beyond = [line_peer(d)[1] for d in (2, NZ - 2)]
    pl.semaphore_signal(barrier, inc=1, device_id=(me, other), device_id_type=MESH)
    for pts in (*ring, *column, *beyond, *beside):
        pl.semaphore_signal(barrier, inc=1, device_id=(pts, c), device_id_type=MESH)

    def load(piece):
        span = points // PIECES
        spots = pl.ds(piece * span, span)
        return pltpu.make_async_copy(
            greens_ref.at[:, :, spots], g_all.at[c, :, :, spots], load_sem.at[piece]
        )

    for piece in range(PIECES):
        load(piece).start()
    load_source = pltpu.make_async_copy(source_hbm, source_ref, local_sem.at[1])
    load_source.start()

    def exchange(piece):
        span = points // PIECES
        spots = pl.ds(piece * span, span)
        return pltpu.make_async_remote_copy(
            src_ref=g_all.at[c, :, :, spots],
            dst_ref=g_all.at[c, :, :, spots],
            send_sem=gx_send.at[piece],
            recv_sem=gx_recv.at[piece],
            device_id=(me, other),
            device_id_type=MESH,
        )

    load_ids = pltpu.make_async_copy(ids_hbm, ids_ref, local_sem.at[2])
    load_ids.start()
    load_obs = pltpu.make_async_copy(
        observed_ref.at[part_k, :, :, pl.ds(row_k, ROWS), :], obs_buf, local_sem.at[3]
    )
    load_obs.start()
    load_mask = pltpu.make_async_copy(
        mask_ref.at[:, :, pl.ds(row_k, ROWS), :], mask_buf, local_sem.at[4]
    )
    load_mask.start()

    def rs_copy(chunk, d):
        peer, peer_pts = plane_peer(d)
        return pltpu.make_async_remote_copy(
            src_ref=part_bufs[chunk].at[peer],
            dst_ref=rs_bufs[chunk].at[d],
            send_sem=rs_send.at[chunk, d],
            recv_sem=rs_recv.at[chunk, d],
            device_id=(peer_pts, c),
            device_id_type=MESH,
        )

    def zx_copy(chunk, d, slot):
        return pltpu.make_async_remote_copy(
            src_ref=zx_bufs[chunk].at[slot],
            dst_ref=zx_bufs[chunk].at[slot],
            send_sem=zx_send.at[chunk, d],
            recv_sem=zx_recv.at[chunk, d],
            device_id=(line_peer(d)[1], c),
            device_id_type=MESH,
        )

    def half_of(chunk):
        return (c + CHUNKS[chunk][0]) % 2

    def ag_copy(chunk, d, owner):
        _, first, subs = CHUNKS[chunk]
        rows = pl.multiple_of((owner % GROUPS) * ROWS, ROWS)
        block = adj.at[
            owner // GROUPS, half_of(chunk), pl.ds(first, subs), pl.ds(rows, ROWS), :
        ]
        return pltpu.make_async_remote_copy(
            src_ref=block,
            dst_ref=block,
            send_sem=ag_send.at[chunk, d],
            recv_sem=ag_recv.at[chunk, d],
            device_id=(plane_peer(d)[1], c),
            device_id_type=MESH,
        )

    def correlate(chunk):
        half = half_of(chunk)
        real = jnp.zeros((HALF, HALF), jnp.float32)
        imag = jnp.zeros((HALF, HALF), jnp.float32)
        span = points // PIECES
        for piece in range(PIECES):
            if chunk > 0:
                exchange(piece).wait_recv()
            spots = pl.ds(piece * span, span)
            rows_re = g_all[half, 0, :, spots]
            rows_im = g_all[half, 1, :, spots]
            own_re = weighted[0, :, spots]
            own_im = weighted[1, :, spots]
            real += dot_nt(rows_re, own_re) + dot_nt(rows_im, own_im)
            imag += dot_nt(rows_im, own_re) - dot_nt(rows_re, own_im)
        for part, value in enumerate((real, imag)):
            for sub in range(2):
                block = value[sub * SUB : (sub + 1) * SUB].astype(jnp.bfloat16)
                part_bufs[chunk][part * GROUPS : (part + 1) * GROUPS, sub] = block.reshape(
                    GROUPS, ROWS, HALF
                )

    def scatter(chunk, peers=PLANE_PEERS):
        for dy, dx in peers:
            rs_copy(chunk, dy * NX + dx).start()

    def reduce_plane(chunk):
        def add(d, total):
            rs_copy(chunk, d).wait_recv()
            return total + rs_bufs[chunk][d].astype(jnp.float32)

        total = lax.fori_loop(1, PLANE, add, part_bufs[chunk][k].astype(jnp.float32))
        zx_bufs[chunk][z] = total.astype(jnp.bfloat16)
        for d in LINE_PEERS:
            zx_copy(chunk, d, z).start()

    def make_adjoint(chunk):
        _, first, subs = CHUNKS[chunk]
        each(1, NZ, lambda d: zx_copy(chunk, d, (z - d + NZ) % NZ).wait_recv())
        half = half_of(chunk)
        corr = zx_bufs[chunk][0].astype(jnp.float32)
        for slot in range(1, NZ):
            corr = corr + zx_bufs[chunk][slot].astype(jnp.float32)
        for sub in range(subs):
            value = kept[half, first + sub] * (
                norm_factor * corr[sub] - obs_buf[half, first + sub]
            )
            adj[part_k, half, first + sub, pl.ds(row_k, ROWS), :] = value.astype(
                jnp.bfloat16
            )
        for dy, dx in PLANE_PEERS:
            ag_copy(chunk, dy * NX + dx, k).start()

    def gather(chunk):
        def wait(d):
            from_y = (y - d // NX + NY) % NY
            from_x = (x - d % NX + NX) % NX
            ag_copy(chunk, d, from_y * NX + from_x).wait_recv()

        each(1, PLANE, wait)

    def store(chunk):
        _, first, subs = CHUNKS[chunk]
        half = half_of(chunk)
        return pltpu.make_async_copy(
            adj.at[:, half, pl.ds(first, subs)],
            adjoint_ref.at[:, half, pl.ds(first, subs)],
            local_sem.at[5 + chunk],
        )

    def swap(piece):
        spots = pl.ds(piece * WIDTH, WIDTH)
        return pltpu.make_async_remote_copy(
            src_ref=k_own.at[:, spots],
            dst_ref=k_other.at[:, spots],
            send_sem=kx_send.at[piece],
            recv_sem=kx_recv.at[piece],
            device_id=(me, other),
            device_id_type=MESH,
        )

    def wave(chunk):
        _, first, subs = CHUNKS[chunk]
        half = half_of(chunk)
        count_rows = subs * SUB
        rows = pl.ds(first * SUB, count_rows)
        res_re = adj[0, half, first : first + subs].reshape(count_rows, HALF)
        res_im = adj[1, half, first : first + subs].reshape(count_rows, HALF)
        for piece in range(points // WIDTH):
            spots = pl.ds(piece * WIDTH, WIDTH)
            own_re = g_all[c, 0, :, spots]
            own_im = g_all[c, 1, :, spots]
            real = dot_nn(res_re, own_re) - dot_nn(res_im, own_im)
            imag = dot_nn(res_re, own_im) + dot_nn(res_im, own_re)
            row_re = g_all[half, 0, rows, spots].astype(jnp.float32)
            row_im = g_all[half, 1, rows, spots].astype(jnp.float32)
            terms = real * row_re + imag * row_im
            terms = jnp.sum(terms.reshape(count_rows // 8, 8, WIDTH), axis=0)
            if chunk > 0:
                terms = terms + k_acc[:, spots]
            if chunk < count - 1:
                k_acc[:, spots] = terms
            else:
                k_own[:, spots] = norm_factor * jnp.sum(terms, axis=0, keepdims=True)
                swap(piece).start()

    pl.semaphore_wait(barrier, 1 + len(ring) + len(column) + len(beside) + len(beyond))
    for piece in range(PIECES):
        load(piece).wait()
        exchange(piece).start()
    for pts in (*ring, *beyond):
        pl.semaphore_signal(known, inc=1, device_id=(pts, c), device_id_type=MESH)
    load_source.wait()
    source = source_ref[...]
    weighted[0] = (source * g_all[c, 0].astype(jnp.float32)).astype(jnp.bfloat16)
    weighted[1] = (source * g_all[c, 1].astype(jnp.float32)).astype(jnp.bfloat16)

    correlate(0)
    scatter(0, [(dy, dx) for dy, dx in PLANE_PEERS if dy * dx == 0])

    load_ids.wait()
    load_mask.wait()
    load_obs.wait()
    ids = ids_ref[...].astype(jnp.float32)
    stations = ids.shape[1]
    col_ids = ids_ref[:, pl.ds(pl.multiple_of(c * HALF, HALF), HALF)].astype(jnp.float32)
    spot = lax.broadcasted_iota(jnp.int32, (ROWS, stations), 1)
    row = lax.broadcasted_iota(jnp.int32, (ROWS, stations), 0) + row_k
    for half in range(2):
        for sub in range(2):
            here = spot == row + (half * HALF + sub * SUB)
            row_ids = jnp.sum(jnp.where(here, ids, 0.0), axis=1, keepdims=True)
            keep = (mask_buf[half, sub] == 1) & (row_ids != col_ids)
            kept[half, sub] = jnp.where(keep, 1.0, 0.0)

    pl.semaphore_wait(known, len(ring) + len(beyond))
    scatter(0, [(dy, dx) for dy, dx in PLANE_PEERS if dy * dx != 0])
    for chunk in range(1, count):
        correlate(chunk)
        scatter(chunk)
    for chunk in range(count):
        reduce_plane(chunk)
    for piece in range(PIECES):
        exchange(piece).wait_send()
    for chunk in range(count):
        each(1, PLANE, lambda d: rs_copy(chunk, d).wait_send())
    for chunk in range(count):
        make_adjoint(chunk)
    for chunk in range(count):
        each(1, NZ, lambda d: zx_copy(chunk, d, z).wait_send())
    for chunk in range(count):
        if chunk == count - 1:
            for sent in range(count - 1):
                each(1, PLANE, lambda d: ag_copy(sent, d, k).wait_send())
        gather(chunk)
        store(chunk).start()
        wave(chunk)

    each(1, PLANE, lambda d: ag_copy(count - 1, d, k).wait_send())
    for chunk in range(count):
        store(chunk).wait()
    for piece in range(points // WIDTH):
        swap(piece).wait()
    kernel_ref[...] = k_own[...] + k_other[...]


def body(greens, source, observed, pair_mask, block_ids):
    own_count, points = greens.shape[1], greens.shape[2]
    stations = observed.shape[1]
    norm_factor = float(points * lax.axis_size("pts")) ** (-0.5)
    vmem = pl.BlockSpec(memory_space=pltpu.VMEM)
    hbm = pl.BlockSpec(memory_space=pltpu.HBM)
    anywhere = pl.BlockSpec(memory_space=pl.ANY)
    dma = pltpu.SemaphoreType.DMA
    bf16, f32 = jnp.bfloat16, jnp.float32
    count = len(CHUNKS)
    pieces = points // WIDTH

    def blocks(slots):
        return [pltpu.VMEM((slots, subs, ROWS, HALF), bf16) for _, _, subs in CHUNKS]

    operands = (
        greens,
        source.reshape(1, points),
        observed.reshape(2, 2, 2, SUB, HALF),
        pair_mask.reshape(2, 2, SUB, HALF),
        block_ids.reshape(1, stations),
    )
    kernel, adjoint = pl.pallas_call(
        functools.partial(kernel_body, norm_factor),
        out_shape=(
            jax.ShapeDtypeStruct((1, points), f32),
            jax.ShapeDtypeStruct((2, 2, 2, SUB, HALF), bf16),
        ),
        in_specs=[hbm] * 5,
        out_specs=(vmem, anywhere),
        scratch_shapes=[
            pltpu.VMEM((2, 2, HALF, points), bf16),
            pltpu.VMEM((2, HALF, points), bf16),
            pltpu.VMEM((2, 2, 2, SUB, HALF), bf16),
            pltpu.VMEM((2, 2, ROWS, HALF), f32),
            pltpu.VMEM((2, 2, ROWS, HALF), jnp.int32),
            pltpu.VMEM((2, 2, ROWS, HALF), f32),
            pltpu.VMEM((1, points), f32),
            pltpu.VMEM((1, stations), jnp.int32),
            pltpu.VMEM((8, points), f32),
            pltpu.VMEM((1, points), f32),
            pltpu.VMEM((1, points), f32),
            pltpu.SemaphoreType.REGULAR,
            dma((PIECES,)),
            dma((5 + count,)),
            dma((PIECES,)),
            dma((PIECES,)),
            dma((count, PLANE)),
            dma((count, PLANE)),
            dma((count, NZ)),
            dma((count, NZ)),
            dma((count, PLANE)),
            dma((count, PLANE)),
            dma((pieces,)),
            dma((pieces,)),
            *blocks(PLANE),
            *blocks(PLANE),
            *blocks(NZ),
        ],
        compiler_params=pltpu.CompilerParams(
            collective_id=0, has_side_effects=True, vmem_limit_bytes=48 * 2**20
        ),
        cost_estimate=pl.CostEstimate(
            flops=16 * stations * own_count * points,
            bytes_accessed=8 * 2**20,
            transcendentals=0,
        ),
        name="noise_kernel",
    )(*(pltpu.with_memory_space_constraint(operand, pltpu.HBM) for operand in operands))
    return kernel.reshape(points), adjoint.reshape(2, stations, own_count)


def solution(mesh):
    placed = (P(None, "sta", "pts"), P("pts"), P(None, None, "sta"), P(None, "sta"), P())
    return jax.shard_map(
        body,
        mesh=mesh,
        in_specs=placed,
        out_specs=(P("pts"), P(None, None, "sta")),
        check_vma=False,
    )
```

```python
import functools

import jax
import jax.numpy as jnp
from jax import lax
from jax.experimental import pallas as pl
from jax.experimental.pallas import tpu as pltpu
from jax.sharding import PartitionSpec as P

NY, NZ, NX = 4, 8, 4
PLANE = NY * NX
HALF = 256
SUB = 128
ROWS = 16
GROUPS = SUB // ROWS
WIDTH = 2048
CHUNKS = ((0, 0, 2), (1, 0, 2))
PIECES = 4
MESH = pl.DeviceIdType.MESH
PLANE_PEERS = (
    (2, 2), (3, 2), (2, 3), (1, 2), (2, 1), (0, 2), (2, 0), (3, 1),
    (1, 3), (3, 3), (1, 1), (3, 0), (0, 3), (1, 0), (0, 1),
)
LINE_PEERS = (4, 3, 5, 2, 6, 1, 7)


def dot_nt(left, right):
    return lax.dot_general(
        left, right, (((1,), (1,)), ((), ())), preferred_element_type=jnp.float32
    )


def dot_nn(left, right):
    return lax.dot_general(
        left, right, (((1,), (0,)), ((), ())), preferred_element_type=jnp.float32
    )


def kernel_body(
    norm_factor,
    greens_ref,
    source_hbm,
    observed_ref,
    mask_ref,
    ids_hbm,
    kernel_ref,
    adjoint_ref,
    g_all,
    weighted,
    adj,
    obs_buf,
    mask_buf,
    kept,
    source_ref,
    ids_ref,
    k_acc,
    k_own,
    k_other,
    known,
    load_sem,
    local_sem,
    gx_send,
    gx_recv,
    rs_send,
    rs_recv,
    zx_send,
    zx_recv,
    ag_send,
    ag_recv,
    kx_send,
    kx_recv,
    *buffers,
):
    count = len(CHUNKS)
    part_bufs = buffers[:count]
    rs_bufs = buffers[count : 2 * count]
    zx_bufs = buffers[2 * count :]
    points = greens_ref.shape[2]
    me = lax.axis_index("pts")
    c = lax.axis_index("sta")
    other = 1 - c
    x = me % NX
    z = (me // NX) % NZ
    y = me // (NX * NZ)
    k = y * NX + x
    part_k = k // GROUPS
    row_k = pl.multiple_of((k % GROUPS) * ROWS, ROWS)

    def plane_peer(d):
        py = (y + d // NX) % NY
        px = (x + d % NX) % NX
        return py * NX + px, (py * NZ + z) * NX + px

    def line_peer(d):
        pz = (z + d) % NZ
        return pz, (y * NZ + pz) * NX + x

    def each(start, stop, step):
        def once(d, carry):
            step(d)
            return carry

        lax.fori_loop(start, stop, once, 0)

    barrier = pltpu.get_barrier_semaphore()
    ring = [plane_peer(d)[1] for d in range(1, NX)]
    column = [plane_peer(d * NX)[1] for d in range(1, NY)]
    beside = [line_peer(d)[1] for d in (1, NZ - 1)]
    beyond = [line_peer(d)[1] for d in (2, NZ - 2)]
    pl.semaphore_signal(barrier, inc=1, device_id=(me, other), device_id_type=MESH)
    for pts in (*ring, *column, *beyond, *beside):
        pl.semaphore_signal(barrier, inc=1, device_id=(pts, c), device_id_type=MESH)

    def load(piece):
        span = points // PIECES
        spots = pl.ds(piece * span, span)
        return pltpu.make_async_copy(
            greens_ref.at[:, :, spots], g_all.at[c, :, :, spots], load_sem.at[piece]
        )

    for piece in range(PIECES):
        load(piece).start()
    load_source = pltpu.make_async_copy(source_hbm, source_ref, local_sem.at[1])
    load_source.start()

    def exchange(piece):
        span = points // PIECES
        spots = pl.ds(piece * span, span)
        return pltpu.make_async_remote_copy(
            src_ref=g_all.at[c, :, :, spots],
            dst_ref=g_all.at[c, :, :, spots],
            send_sem=gx_send.at[piece],
            recv_sem=gx_recv.at[piece],
            device_id=(me, other),
            device_id_type=MESH,
        )

    load_ids = pltpu.make_async_copy(ids_hbm, ids_ref, local_sem.at[2])
    load_ids.start()
    load_obs = pltpu.make_async_copy(
        observed_ref.at[part_k, :, :, pl.ds(row_k, ROWS), :], obs_buf, local_sem.at[3]
    )
    load_obs.start()
    load_mask = pltpu.make_async_copy(
        mask_ref.at[:, :, pl.ds(row_k, ROWS), :], mask_buf, local_sem.at[4]
    )
    load_mask.start()

    def rs_copy(chunk, d):
        peer, peer_pts = plane_peer(d)
        return pltpu.make_async_remote_copy(
            src_ref=part_bufs[chunk].at[peer],
            dst_ref=rs_bufs[chunk].at[d],
            send_sem=rs_send.at[chunk, d],
            recv_sem=rs_recv.at[chunk, d],
            device_id=(peer_pts, c),
            device_id_type=MESH,
        )

    def zx_copy(chunk, d, slot):
        return pltpu.make_async_remote_copy(
            src_ref=zx_bufs[chunk].at[slot],
            dst_ref=zx_bufs[chunk].at[slot],
            send_sem=zx_send.at[chunk, d],
            recv_sem=zx_recv.at[chunk, d],
            device_id=(line_peer(d)[1], c),
            device_id_type=MESH,
        )

    def half_of(chunk):
        return (c + CHUNKS[chunk][0]) % 2

    def ag_copy(chunk, d, owner):
        _, first, subs = CHUNKS[chunk]
        rows = pl.multiple_of((owner % GROUPS) * ROWS, ROWS)
        block = adj.at[
            owner // GROUPS, half_of(chunk), pl.ds(first, subs), pl.ds(rows, ROWS), :
        ]
        return pltpu.make_async_remote_copy(
            src_ref=block,
            dst_ref=block,
            send_sem=ag_send.at[chunk, d],
            recv_sem=ag_recv.at[chunk, d],
            device_id=(plane_peer(d)[1], c),
            device_id_type=MESH,
        )

    def correlate(chunk):
        half = half_of(chunk)
        real = jnp.zeros((HALF, HALF), jnp.float32)
        imag = jnp.zeros((HALF, HALF), jnp.float32)
        span = points // PIECES
        for piece in range(PIECES):
            if chunk > 0:
                exchange(piece).wait_recv()
            spots = pl.ds(piece * span, span)
            rows_re = g_all[half, 0, :, spots]
            rows_im = g_all[half, 1, :, spots]
            own_re = weighted[0, :, spots]
            own_im = weighted[1, :, spots]
            real += dot_nt(rows_re, own_re) + dot_nt(rows_im, own_im)
            imag += dot_nt(rows_im, own_re) - dot_nt(rows_re, own_im)
        for part, value in enumerate((real, imag)):
            for sub in range(2):
                block = value[sub * SUB : (sub + 1) * SUB].astype(jnp.bfloat16)
                part_bufs[chunk][part * GROUPS : (part + 1) * GROUPS, sub] = block.reshape(
                    GROUPS, ROWS, HALF
                )

    def scatter(chunk, peers=PLANE_PEERS):
        for dy, dx in peers:
            rs_copy(chunk, dy * NX + dx).start()

    def reduce_plane(chunk):
        def add(d, total):
            rs_copy(chunk, d).wait_recv()
            return total + rs_bufs[chunk][d].astype(jnp.float32)

        total = lax.fori_loop(1, PLANE, add, part_bufs[chunk][k].astype(jnp.float32))
        zx_bufs[chunk][z] = total.astype(jnp.bfloat16)
        for d in LINE_PEERS:
            zx_copy(chunk, d, z).start()

    def make_adjoint(chunk):
        _, first, subs = CHUNKS[chunk]
        each(1, NZ, lambda d: zx_copy(chunk, d, (z - d + NZ) % NZ).wait_recv())
        half = half_of(chunk)
        corr = zx_bufs[chunk][0].astype(jnp.float32)
        for slot in range(1, NZ):
            corr = corr + zx_bufs[chunk][slot].astype(jnp.float32)
        for sub in range(subs):
            value = kept[half, first + sub] * (
                norm_factor * corr[sub] - obs_buf[half, first + sub]
            )
            adj[part_k, half, first + sub, pl.ds(row_k, ROWS), :] = value.astype(
                jnp.bfloat16
            )
        for dy, dx in PLANE_PEERS:
            ag_copy(chunk, dy * NX + dx, k).start()

    def gather(chunk):
        def wait(d):
            from_y = (y - d // NX + NY) % NY
            from_x = (x - d % NX + NX) % NX
            ag_copy(chunk, d, from_y * NX + from_x).wait_recv()

        each(1, PLANE, wait)

    def store(chunk):
        _, first, subs = CHUNKS[chunk]
        half = half_of(chunk)
        return pltpu.make_async_copy(
            adj.at[:, half, pl.ds(first, subs)],
            adjoint_ref.at[:, half, pl.ds(first, subs)],
            local_sem.at[5 + chunk],
        )

    def swap(piece):
        spots = pl.ds(piece * WIDTH, WIDTH)
        return pltpu.make_async_remote_copy(
            src_ref=k_own.at[:, spots],
            dst_ref=k_other.at[:, spots],
            send_sem=kx_send.at[piece],
            recv_sem=kx_recv.at[piece],
            device_id=(me, other),
            device_id_type=MESH,
        )

    def wave(chunk):
        _, first, subs = CHUNKS[chunk]
        half = half_of(chunk)
        count_rows = subs * SUB
        rows = pl.ds(first * SUB, count_rows)
        res_re = adj[0, half, first : first + subs].reshape(count_rows, HALF)
        res_im = adj[1, half, first : first + subs].reshape(count_rows, HALF)
        for piece in range(points // WIDTH):
            spots = pl.ds(piece * WIDTH, WIDTH)
            own_re = g_all[c, 0, :, spots]
            own_im = g_all[c, 1, :, spots]
            real = dot_nn(res_re, own_re) - dot_nn(res_im, own_im)
            imag = dot_nn(res_re, own_im) + dot_nn(res_im, own_re)
            row_re = g_all[half, 0, rows, spots].astype(jnp.float32)
            row_im = g_all[half, 1, rows, spots].astype(jnp.float32)
            terms = real * row_re + imag * row_im
            terms = jnp.sum(terms.reshape(count_rows // 8, 8, WIDTH), axis=0)
            if chunk > 0:
                terms = terms + k_acc[:, spots]
            if chunk < count - 1:
                k_acc[:, spots] = terms
            else:
                k_own[:, spots] = norm_factor * jnp.sum(terms, axis=0, keepdims=True)
                swap(piece).start()

    pl.semaphore_wait(barrier, 1 + len(ring) + len(column) + len(beside) + len(beyond))
    for piece in range(PIECES):
        load(piece).wait()
        exchange(piece).start()
    for pts in (*ring, *beyond):
        pl.semaphore_signal(known, inc=1, device_id=(pts, c), device_id_type=MESH)
    load_source.wait()
    source = source_ref[...]
    weighted[0] = (source * g_all[c, 0].astype(jnp.float32)).astype(jnp.bfloat16)
    weighted[1] = (source * g_all[c, 1].astype(jnp.float32)).astype(jnp.bfloat16)

    correlate(0)

    load_ids.wait()
    load_mask.wait()
    load_obs.wait()
    ids = ids_ref[...].astype(jnp.float32)
    stations = ids.shape[1]
    col_ids = ids_ref[:, pl.ds(pl.multiple_of(c * HALF, HALF), HALF)].astype(jnp.float32)
    spot = lax.broadcasted_iota(jnp.int32, (ROWS, stations), 1)
    row = lax.broadcasted_iota(jnp.int32, (ROWS, stations), 0) + row_k
    for half in range(2):
        for sub in range(2):
            here = spot == row + (half * HALF + sub * SUB)
            row_ids = jnp.sum(jnp.where(here, ids, 0.0), axis=1, keepdims=True)
            keep = (mask_buf[half, sub] == 1) & (row_ids != col_ids)
            kept[half, sub] = jnp.where(keep, 1.0, 0.0)

    pl.semaphore_wait(known, len(ring) + len(beyond))
    scatter(0)
    for chunk in range(1, count):
        correlate(chunk)
        scatter(chunk)
    for chunk in range(count):
        reduce_plane(chunk)
    for piece in range(PIECES):
        exchange(piece).wait_send()
    for chunk in range(count):
        each(1, PLANE, lambda d: rs_copy(chunk, d).wait_send())
    for chunk in range(count):
        make_adjoint(chunk)
    for chunk in range(count):
        each(1, NZ, lambda d: zx_copy(chunk, d, z).wait_send())
    for chunk in range(count):
        if chunk == count - 1:
            for sent in range(count - 1):
                each(1, PLANE, lambda d: ag_copy(sent, d, k).wait_send())
        gather(chunk)
        store(chunk).start()
        wave(chunk)

    each(1, PLANE, lambda d: ag_copy(count - 1, d, k).wait_send())
    for chunk in range(count):
        store(chunk).wait()
    for piece in range(points // WIDTH):
        swap(piece).wait()
    kernel_ref[...] = k_own[...] + k_other[...]


def body(greens, source, observed, pair_mask, block_ids):
    own_count, points = greens.shape[1], greens.shape[2]
    stations = observed.shape[1]
    norm_factor = float(points * lax.axis_size("pts")) ** (-0.5)
    vmem = pl.BlockSpec(memory_space=pltpu.VMEM)
    hbm = pl.BlockSpec(memory_space=pltpu.HBM)
    anywhere = pl.BlockSpec(memory_space=pl.ANY)
    dma = pltpu.SemaphoreType.DMA
    bf16, f32 = jnp.bfloat16, jnp.float32
    count = len(CHUNKS)
    pieces = points // WIDTH

    def blocks(slots):
        return [pltpu.VMEM((slots, subs, ROWS, HALF), bf16) for _, _, subs in CHUNKS]

    operands = (
        greens,
        source.reshape(1, points),
        observed.reshape(2, 2, 2, SUB, HALF),
        pair_mask.reshape(2, 2, SUB, HALF),
        block_ids.reshape(1, stations),
    )
    kernel, adjoint = pl.pallas_call(
        functools.partial(kernel_body, norm_factor),
        out_shape=(
            jax.ShapeDtypeStruct((1, points), f32),
            jax.ShapeDtypeStruct((2, 2, 2, SUB, HALF), bf16),
        ),
        in_specs=[hbm] * 5,
        out_specs=(vmem, anywhere),
        scratch_shapes=[
            pltpu.VMEM((2, 2, HALF, points), bf16),
            pltpu.VMEM((2, HALF, points), bf16),
            pltpu.VMEM((2, 2, 2, SUB, HALF), bf16),
            pltpu.VMEM((2, 2, ROWS, HALF), f32),
            pltpu.VMEM((2, 2, ROWS, HALF), jnp.int32),
            pltpu.VMEM((2, 2, ROWS, HALF), f32),
            pltpu.VMEM((1, points), f32),
            pltpu.VMEM((1, stations), jnp.int32),
            pltpu.VMEM((8, points), f32),
            pltpu.VMEM((1, points), f32),
            pltpu.VMEM((1, points), f32),
            pltpu.SemaphoreType.REGULAR,
            dma((PIECES,)),
            dma((5 + count,)),
            dma((PIECES,)),
            dma((PIECES,)),
            dma((count, PLANE)),
            dma((count, PLANE)),
            dma((count, NZ)),
            dma((count, NZ)),
            dma((count, PLANE)),
            dma((count, PLANE)),
            dma((pieces,)),
            dma((pieces,)),
            *blocks(PLANE),
            *blocks(PLANE),
            *blocks(NZ),
        ],
        compiler_params=pltpu.CompilerParams(
            collective_id=0, has_side_effects=True, vmem_limit_bytes=48 * 2**20
        ),
        cost_estimate=pl.CostEstimate(
            flops=16 * stations * own_count * points,
            bytes_accessed=8 * 2**20,
            transcendentals=0,
        ),
        name="noise_kernel",
    )(*(pltpu.with_memory_space_constraint(operand, pltpu.HBM) for operand in operands))
    return kernel.reshape(points), adjoint.reshape(2, stations, own_count)


def solution(mesh):
    placed = (P(None, "sta", "pts"), P("pts"), P(None, None, "sta"), P(None, "sta"), P())
    return jax.shard_map(
        body,
        mesh=mesh,
        in_specs=placed,
        out_specs=(P("pts"), P(None, None, "sta")),
        check_vma=False,
    )
```

```python
import functools

import jax
import jax.numpy as jnp
from jax import lax
from jax.experimental import pallas as pl
from jax.experimental.pallas import tpu as pltpu
from jax.sharding import PartitionSpec as P

NY, NZ, NX = 4, 8, 4
PLANE = NY * NX
HALF = 256
SUB = 128
ROWS = 16
GROUPS = SUB // ROWS
WIDTH = 2048
CHUNKS = ((0, 0, 2), (1, 0, 2))
PIECES = 8
MESH = pl.DeviceIdType.MESH
PLANE_PEERS = (
    (2, 2), (3, 2), (2, 3), (1, 2), (2, 1), (0, 2), (2, 0), (3, 1),
    (1, 3), (3, 3), (1, 1), (3, 0), (0, 3), (1, 0), (0, 1),
)
LINE_PEERS = (4, 3, 5, 2, 6, 1, 7)


def dot_nt(left, right):
    return lax.dot_general(
        left, right, (((1,), (1,)), ((), ())), preferred_element_type=jnp.float32
    )


def dot_nn(left, right):
    return lax.dot_general(
        left, right, (((1,), (0,)), ((), ())), preferred_element_type=jnp.float32
    )


def kernel_body(
    norm_factor,
    greens_ref,
    source_hbm,
    observed_ref,
    mask_ref,
    ids_hbm,
    kernel_ref,
    adjoint_ref,
    g_all,
    weighted,
    adj,
    obs_buf,
    mask_buf,
    kept,
    source_ref,
    ids_ref,
    k_acc,
    k_own,
    k_other,
    known,
    load_sem,
    local_sem,
    gx_send,
    gx_recv,
    rs_send,
    rs_recv,
    zx_send,
    zx_recv,
    ag_send,
    ag_recv,
    kx_send,
    kx_recv,
    *buffers,
):
    count = len(CHUNKS)
    part_bufs = buffers[:count]
    rs_bufs = buffers[count : 2 * count]
    zx_bufs = buffers[2 * count :]
    points = greens_ref.shape[2]
    me = lax.axis_index("pts")
    c = lax.axis_index("sta")
    other = 1 - c
    x = me % NX
    z = (me // NX) % NZ
    y = me // (NX * NZ)
    k = y * NX + x
    part_k = k // GROUPS
    row_k = pl.multiple_of((k % GROUPS) * ROWS, ROWS)

    def plane_peer(d):
        py = (y + d // NX) % NY
        px = (x + d % NX) % NX
        return py * NX + px, (py * NZ + z) * NX + px

    def line_peer(d):
        pz = (z + d) % NZ
        return pz, (y * NZ + pz) * NX + x

    def each(start, stop, step):
        def once(d, carry):
            step(d)
            return carry

        lax.fori_loop(start, stop, once, 0)

    barrier = pltpu.get_barrier_semaphore()
    ring = [plane_peer(d)[1] for d in range(1, NX)]
    column = [plane_peer(d * NX)[1] for d in range(1, NY)]
    beside = [line_peer(d)[1] for d in (1, NZ - 1)]
    beyond = [line_peer(d)[1] for d in (2, NZ - 2)]
    pl.semaphore_signal(barrier, inc=1, device_id=(me, other), device_id_type=MESH)
    for pts in (*ring, *column, *beyond, *beside):
        pl.semaphore_signal(barrier, inc=1, device_id=(pts, c), device_id_type=MESH)

    def load(piece):
        span = points // PIECES
        spots = pl.ds(piece * span, span)
        return pltpu.make_async_copy(
            greens_ref.at[:, :, spots], g_all.at[c, :, :, spots], load_sem.at[piece]
        )

    for piece in range(PIECES):
        load(piece).start()
    load_source = pltpu.make_async_copy(source_hbm, source_ref, local_sem.at[1])
    load_source.start()

    def exchange(piece):
        span = points // PIECES
        spots = pl.ds(piece * span, span)
        return pltpu.make_async_remote_copy(
            src_ref=g_all.at[c, :, :, spots],
            dst_ref=g_all.at[c, :, :, spots],
            send_sem=gx_send.at[piece],
            recv_sem=gx_recv.at[piece],
            device_id=(me, other),
            device_id_type=MESH,
        )

    load_ids = pltpu.make_async_copy(ids_hbm, ids_ref, local_sem.at[2])
    load_ids.start()
    load_obs = pltpu.make_async_copy(
        observed_ref.at[part_k, :, :, pl.ds(row_k, ROWS), :], obs_buf, local_sem.at[3]
    )
    load_obs.start()
    load_mask = pltpu.make_async_copy(
        mask_ref.at[:, :, pl.ds(row_k, ROWS), :], mask_buf, local_sem.at[4]
    )
    load_mask.start()

    def rs_copy(chunk, d):
        peer, peer_pts = plane_peer(d)
        return pltpu.make_async_remote_copy(
            src_ref=part_bufs[chunk].at[peer],
            dst_ref=rs_bufs[chunk].at[d],
            send_sem=rs_send.at[chunk, d],
            recv_sem=rs_recv.at[chunk, d],
            device_id=(peer_pts, c),
            device_id_type=MESH,
        )

    def zx_copy(chunk, d, slot):
        return pltpu.make_async_remote_copy(
            src_ref=zx_bufs[chunk].at[slot],
            dst_ref=zx_bufs[chunk].at[slot],
            send_sem=zx_send.at[chunk, d],
            recv_sem=zx_recv.at[chunk, d],
            device_id=(line_peer(d)[1], c),
            device_id_type=MESH,
        )

    def half_of(chunk):
        return (c + CHUNKS[chunk][0]) % 2

    def ag_copy(chunk, d, owner):
        _, first, subs = CHUNKS[chunk]
        rows = pl.multiple_of((owner % GROUPS) * ROWS, ROWS)
        block = adj.at[
            owner // GROUPS, half_of(chunk), pl.ds(first, subs), pl.ds(rows, ROWS), :
        ]
        return pltpu.make_async_remote_copy(
            src_ref=block,
            dst_ref=block,
            send_sem=ag_send.at[chunk, d],
            recv_sem=ag_recv.at[chunk, d],
            device_id=(plane_peer(d)[1], c),
            device_id_type=MESH,
        )

    def correlate(chunk):
        half = half_of(chunk)
        real = jnp.zeros((HALF, HALF), jnp.float32)
        imag = jnp.zeros((HALF, HALF), jnp.float32)
        span = points // PIECES
        for piece in range(PIECES):
            if chunk > 0:
                exchange(piece).wait_recv()
            spots = pl.ds(piece * span, span)
            rows_re = g_all[half, 0, :, spots]
            rows_im = g_all[half, 1, :, spots]
            own_re = weighted[0, :, spots]
            own_im = weighted[1, :, spots]
            real += dot_nt(rows_re, own_re) + dot_nt(rows_im, own_im)
            imag += dot_nt(rows_im, own_re) - dot_nt(rows_re, own_im)
        for part, value in enumerate((real, imag)):
            for sub in range(2):
                block = value[sub * SUB : (sub + 1) * SUB].astype(jnp.bfloat16)
                part_bufs[chunk][part * GROUPS : (part + 1) * GROUPS, sub] = block.reshape(
                    GROUPS, ROWS, HALF
                )

    def scatter(chunk, peers=PLANE_PEERS):
        for dy, dx in peers:
            rs_copy(chunk, dy * NX + dx).start()

    def reduce_plane(chunk):
        def add(d, total):
            rs_copy(chunk, d).wait_recv()
            return total + rs_bufs[chunk][d].astype(jnp.float32)

        total = lax.fori_loop(1, PLANE, add, part_bufs[chunk][k].astype(jnp.float32))
        zx_bufs[chunk][z] = total.astype(jnp.bfloat16)
        for d in LINE_PEERS:
            zx_copy(chunk, d, z).start()

    def make_adjoint(chunk):
        _, first, subs = CHUNKS[chunk]
        each(1, NZ, lambda d: zx_copy(chunk, d, (z - d + NZ) % NZ).wait_recv())
        half = half_of(chunk)
        corr = zx_bufs[chunk][0].astype(jnp.float32)
        for slot in range(1, NZ):
            corr = corr + zx_bufs[chunk][slot].astype(jnp.float32)
        for sub in range(subs):
            value = kept[half, first + sub] * (
                norm_factor * corr[sub] - obs_buf[half, first + sub]
            )
            adj[part_k, half, first + sub, pl.ds(row_k, ROWS), :] = value.astype(
                jnp.bfloat16
            )
        for dy, dx in PLANE_PEERS:
            ag_copy(chunk, dy * NX + dx, k).start()

    def gather(chunk):
        def wait(d):
            from_y = (y - d // NX + NY) % NY
            from_x = (x - d % NX + NX) % NX
            ag_copy(chunk, d, from_y * NX + from_x).wait_recv()

        each(1, PLANE, wait)

    def store(chunk):
        _, first, subs = CHUNKS[chunk]
        half = half_of(chunk)
        return pltpu.make_async_copy(
            adj.at[:, half, pl.ds(first, subs)],
            adjoint_ref.at[:, half, pl.ds(first, subs)],
            local_sem.at[5 + chunk],
        )

    def swap(piece):
        spots = pl.ds(piece * WIDTH, WIDTH)
        return pltpu.make_async_remote_copy(
            src_ref=k_own.at[:, spots],
            dst_ref=k_other.at[:, spots],
            send_sem=kx_send.at[piece],
            recv_sem=kx_recv.at[piece],
            device_id=(me, other),
            device_id_type=MESH,
        )

    def wave(chunk):
        _, first, subs = CHUNKS[chunk]
        half = half_of(chunk)
        count_rows = subs * SUB
        rows = pl.ds(first * SUB, count_rows)
        res_re = adj[0, half, first : first + subs].reshape(count_rows, HALF)
        res_im = adj[1, half, first : first + subs].reshape(count_rows, HALF)
        residual = jnp.concatenate(
            [
                jnp.concatenate([res_re, -res_im], axis=1),
                jnp.concatenate([res_im, res_re], axis=1),
            ],
            axis=0,
        )
        for piece in range(points // WIDTH):
            spots = pl.ds(piece * WIDTH, WIDTH)
            own = g_all[c, :, :, spots].reshape(2 * HALF, WIDTH)
            product = dot_nn(residual, own)
            real, imag = product[:count_rows], product[count_rows:]
            row_re = g_all[half, 0, rows, spots].astype(jnp.float32)
            row_im = g_all[half, 1, rows, spots].astype(jnp.float32)
            terms = real * row_re + imag * row_im
            terms = jnp.sum(terms.reshape(count_rows // 8, 8, WIDTH), axis=0)
            if chunk > 0:
                terms = terms + k_acc[:, spots]
            if chunk < count - 1:
                k_acc[:, spots] = terms
            else:
                k_own[:, spots] = norm_factor * jnp.sum(terms, axis=0, keepdims=True)
                swap(piece).start()

    pl.semaphore_wait(barrier, 1 + len(ring) + len(column) + len(beside) + len(beyond))
    for piece in range(PIECES):
        load(piece).wait()
        exchange(piece).start()
    for pts in (*ring, *beyond):
        pl.semaphore_signal(known, inc=1, device_id=(pts, c), device_id_type=MESH)
    load_source.wait()
    source = source_ref[...]
    weighted[0] = (source * g_all[c, 0].astype(jnp.float32)).astype(jnp.bfloat16)
    weighted[1] = (source * g_all[c, 1].astype(jnp.float32)).astype(jnp.bfloat16)

    correlate(0)

    load_ids.wait()
    load_mask.wait()
    load_obs.wait()
    ids = ids_ref[...].astype(jnp.float32)
    stations = ids.shape[1]
    col_ids = ids_ref[:, pl.ds(pl.multiple_of(c * HALF, HALF), HALF)].astype(jnp.float32)
    spot = lax.broadcasted_iota(jnp.int32, (ROWS, stations), 1)
    row = lax.broadcasted_iota(jnp.int32, (ROWS, stations), 0) + row_k
    for half in range(2):
        for sub in range(2):
            here = spot == row + (half * HALF + sub * SUB)
            row_ids = jnp.sum(jnp.where(here, ids, 0.0), axis=1, keepdims=True)
            keep = (mask_buf[half, sub] == 1) & (row_ids != col_ids)
            kept[half, sub] = jnp.where(keep, 1.0, 0.0)

    pl.semaphore_wait(known, len(ring) + len(beyond))
    scatter(0)
    for chunk in range(1, count):
        correlate(chunk)
        scatter(chunk)
    for chunk in range(count):
        reduce_plane(chunk)
    for piece in range(PIECES):
        exchange(piece).wait_send()
    for chunk in range(count):
        each(1, PLANE, lambda d: rs_copy(chunk, d).wait_send())
    for chunk in range(count):
        make_adjoint(chunk)
    for chunk in range(count):
        each(1, NZ, lambda d: zx_copy(chunk, d, z).wait_send())
    for chunk in range(count):
        if chunk == count - 1:
            for sent in range(count - 1):
                each(1, PLANE, lambda d: ag_copy(sent, d, k).wait_send())
        gather(chunk)
        store(chunk).start()
        wave(chunk)

    each(1, PLANE, lambda d: ag_copy(count - 1, d, k).wait_send())
    for chunk in range(count):
        store(chunk).wait()
    for piece in range(points // WIDTH):
        swap(piece).wait()
    kernel_ref[...] = k_own[...] + k_other[...]


def body(greens, source, observed, pair_mask, block_ids):
    own_count, points = greens.shape[1], greens.shape[2]
    stations = observed.shape[1]
    norm_factor = float(points * lax.axis_size("pts")) ** (-0.5)
    vmem = pl.BlockSpec(memory_space=pltpu.VMEM)
    hbm = pl.BlockSpec(memory_space=pltpu.HBM)
    anywhere = pl.BlockSpec(memory_space=pl.ANY)
    dma = pltpu.SemaphoreType.DMA
    bf16, f32 = jnp.bfloat16, jnp.float32
    count = len(CHUNKS)
    pieces = points // WIDTH

    def blocks(slots):
        return [pltpu.VMEM((slots, subs, ROWS, HALF), bf16) for _, _, subs in CHUNKS]

    operands = (
        greens,
        source.reshape(1, points),
        observed.reshape(2, 2, 2, SUB, HALF),
        pair_mask.reshape(2, 2, SUB, HALF),
        block_ids.reshape(1, stations),
    )
    kernel, adjoint = pl.pallas_call(
        functools.partial(kernel_body, norm_factor),
        out_shape=(
            jax.ShapeDtypeStruct((1, points), f32),
            jax.ShapeDtypeStruct((2, 2, 2, SUB, HALF), bf16),
        ),
        in_specs=[hbm] * 5,
        out_specs=(vmem, anywhere),
        scratch_shapes=[
            pltpu.VMEM((2, 2, HALF, points), bf16),
            pltpu.VMEM((2, HALF, points), bf16),
            pltpu.VMEM((2, 2, 2, SUB, HALF), bf16),
            pltpu.VMEM((2, 2, ROWS, HALF), f32),
            pltpu.VMEM((2, 2, ROWS, HALF), jnp.int32),
            pltpu.VMEM((2, 2, ROWS, HALF), f32),
            pltpu.VMEM((1, points), f32),
            pltpu.VMEM((1, stations), jnp.int32),
            pltpu.VMEM((8, points), f32),
            pltpu.VMEM((1, points), f32),
            pltpu.VMEM((1, points), f32),
            pltpu.SemaphoreType.REGULAR,
            dma((PIECES,)),
            dma((5 + count,)),
            dma((PIECES,)),
            dma((PIECES,)),
            dma((count, PLANE)),
            dma((count, PLANE)),
            dma((count, NZ)),
            dma((count, NZ)),
            dma((count, PLANE)),
            dma((count, PLANE)),
            dma((pieces,)),
            dma((pieces,)),
            *blocks(PLANE),
            *blocks(PLANE),
            *blocks(NZ),
        ],
        compiler_params=pltpu.CompilerParams(
            collective_id=0, has_side_effects=True, vmem_limit_bytes=48 * 2**20
        ),
        cost_estimate=pl.CostEstimate(
            flops=16 * stations * own_count * points,
            bytes_accessed=8 * 2**20,
            transcendentals=0,
        ),
        name="noise_kernel",
    )(*(pltpu.with_memory_space_constraint(operand, pltpu.HBM) for operand in operands))
    return kernel.reshape(points), adjoint.reshape(2, stations, own_count)


def solution(mesh):
    placed = (P(None, "sta", "pts"), P("pts"), P(None, None, "sta"), P(None, "sta"), P())
    return jax.shard_map(
        body,
        mesh=mesh,
        in_specs=placed,
        out_specs=(P("pts"), P(None, None, "sta")),
        check_vma=False,
    )
```

```python
import functools

import jax
import jax.numpy as jnp
from jax import lax
from jax.experimental import pallas as pl
from jax.experimental.pallas import tpu as pltpu
from jax.sharding import PartitionSpec as P

NY, NZ, NX = 4, 8, 4
PLANE = NY * NX
HALF = 256
SUB = 128
ROWS = 16
GROUPS = SUB // ROWS
WIDTH = 1024
CHUNKS = ((0, 0, 2), (1, 0, 2))
PIECES = 8
MESH = pl.DeviceIdType.MESH
PLANE_PEERS = (
    (2, 2), (3, 2), (2, 3), (1, 2), (2, 1), (0, 2), (2, 0), (3, 1),
    (1, 3), (3, 3), (1, 1), (3, 0), (0, 3), (1, 0), (0, 1),
)
LINE_PEERS = (4, 3, 5, 2, 6, 1, 7)


def dot_nt(left, right):
    return lax.dot_general(
        left, right, (((1,), (1,)), ((), ())), preferred_element_type=jnp.float32
    )


def dot_nn(left, right):
    return lax.dot_general(
        left, right, (((1,), (0,)), ((), ())), preferred_element_type=jnp.float32
    )


def kernel_body(
    norm_factor,
    greens_ref,
    source_hbm,
    observed_ref,
    mask_ref,
    ids_hbm,
    kernel_ref,
    adjoint_ref,
    g_all,
    weighted,
    adj,
    obs_buf,
    mask_buf,
    kept,
    source_ref,
    ids_ref,
    k_acc,
    k_own,
    k_other,
    known,
    load_sem,
    local_sem,
    gx_send,
    gx_recv,
    rs_send,
    rs_recv,
    zx_send,
    zx_recv,
    ag_send,
    ag_recv,
    kx_send,
    kx_recv,
    *buffers,
):
    count = len(CHUNKS)
    part_bufs = buffers[:count]
    rs_bufs = buffers[count : 2 * count]
    zx_bufs = buffers[2 * count :]
    points = greens_ref.shape[2]
    me = lax.axis_index("pts")
    c = lax.axis_index("sta")
    other = 1 - c
    x = me % NX
    z = (me // NX) % NZ
    y = me // (NX * NZ)
    k = y * NX + x
    part_k = k // GROUPS
    row_k = pl.multiple_of((k % GROUPS) * ROWS, ROWS)

    def plane_peer(d):
        py = (y + d // NX) % NY
        px = (x + d % NX) % NX
        return py * NX + px, (py * NZ + z) * NX + px

    def line_peer(d):
        pz = (z + d) % NZ
        return pz, (y * NZ + pz) * NX + x

    def each(start, stop, step):
        def once(d, carry):
            step(d)
            return carry

        lax.fori_loop(start, stop, once, 0)

    barrier = pltpu.get_barrier_semaphore()
    ring = [plane_peer(d)[1] for d in (2, 1, 3)]
    column = [plane_peer(d * NX)[1] for d in (2, 1, 3)]
    beside = [line_peer(d)[1] for d in (1, NZ - 1)]
    beyond = [line_peer(d)[1] for d in (2, NZ - 2)]
    for pts in (*beyond, *ring, *column, *beside):
        pl.semaphore_signal(barrier, inc=1, device_id=(pts, c), device_id_type=MESH)
    pl.semaphore_signal(barrier, inc=1, device_id=(me, other), device_id_type=MESH)

    def load(piece):
        span = points // PIECES
        spots = pl.ds(piece * span, span)
        return pltpu.make_async_copy(
            greens_ref.at[:, :, spots], g_all.at[c, :, :, spots], load_sem.at[piece]
        )

    for piece in range(PIECES):
        load(piece).start()
    load_source = pltpu.make_async_copy(source_hbm, source_ref, local_sem.at[1])
    load_source.start()

    def exchange(piece):
        span = points // PIECES
        spots = pl.ds(piece * span, span)
        return pltpu.make_async_remote_copy(
            src_ref=g_all.at[c, :, :, spots],
            dst_ref=g_all.at[c, :, :, spots],
            send_sem=gx_send.at[piece],
            recv_sem=gx_recv.at[piece],
            device_id=(me, other),
            device_id_type=MESH,
        )

    load_ids = pltpu.make_async_copy(ids_hbm, ids_ref, local_sem.at[2])
    load_ids.start()
    load_obs = pltpu.make_async_copy(
        observed_ref.at[part_k, :, :, pl.ds(row_k, ROWS), :], obs_buf, local_sem.at[3]
    )
    load_obs.start()
    load_mask = pltpu.make_async_copy(
        mask_ref.at[:, :, pl.ds(row_k, ROWS), :], mask_buf, local_sem.at[4]
    )
    load_mask.start()

    def rs_copy(chunk, d):
        peer, peer_pts = plane_peer(d)
        return pltpu.make_async_remote_copy(
            src_ref=part_bufs[chunk].at[peer],
            dst_ref=rs_bufs[chunk].at[d],
            send_sem=rs_send.at[chunk, d],
            recv_sem=rs_recv.at[chunk, d],
            device_id=(peer_pts, c),
            device_id_type=MESH,
        )

    def zx_copy(chunk, d, slot):
        return pltpu.make_async_remote_copy(
            src_ref=zx_bufs[chunk].at[slot],
            dst_ref=zx_bufs[chunk].at[slot],
            send_sem=zx_send.at[chunk, d],
            recv_sem=zx_recv.at[chunk, d],
            device_id=(line_peer(d)[1], c),
            device_id_type=MESH,
        )

    def half_of(chunk):
        return (c + CHUNKS[chunk][0]) % 2

    def ag_copy(chunk, d, owner):
        _, first, subs = CHUNKS[chunk]
        rows = pl.multiple_of((owner % GROUPS) * ROWS, ROWS)
        block = adj.at[
            owner // GROUPS, half_of(chunk), pl.ds(first, subs), pl.ds(rows, ROWS), :
        ]
        return pltpu.make_async_remote_copy(
            src_ref=block,
            dst_ref=block,
            send_sem=ag_send.at[chunk, d],
            recv_sem=ag_recv.at[chunk, d],
            device_id=(plane_peer(d)[1], c),
            device_id_type=MESH,
        )

    def correlate(chunk):
        half = half_of(chunk)
        real = jnp.zeros((HALF, HALF), jnp.float32)
        imag = jnp.zeros((HALF, HALF), jnp.float32)
        span = points // PIECES
        for piece in range(PIECES):
            if chunk > 0:
                exchange(piece).wait_recv()
            spots = pl.ds(piece * span, span)
            rows_re = g_all[half, 0, :, spots]
            rows_im = g_all[half, 1, :, spots]
            own_re = weighted[0, :, spots]
            own_im = weighted[1, :, spots]
            real += dot_nt(rows_re, own_re) + dot_nt(rows_im, own_im)
            imag += dot_nt(rows_im, own_re) - dot_nt(rows_re, own_im)
        for part, value in enumerate((real, imag)):
            for sub in range(2):
                block = value[sub * SUB : (sub + 1) * SUB].astype(jnp.bfloat16)
                part_bufs[chunk][part * GROUPS : (part + 1) * GROUPS, sub] = block.reshape(
                    GROUPS, ROWS, HALF
                )

    def scatter(chunk, peers=PLANE_PEERS):
        for dy, dx in peers:
            rs_copy(chunk, dy * NX + dx).start()

    def reduce_plane(chunk):
        def add(d, total):
            rs_copy(chunk, d).wait_recv()
            return total + rs_bufs[chunk][d].astype(jnp.float32)

        total = lax.fori_loop(1, PLANE, add, part_bufs[chunk][k].astype(jnp.float32))
        zx_bufs[chunk][z] = total.astype(jnp.bfloat16)
        for d in LINE_PEERS:
            zx_copy(chunk, d, z).start()

    def make_adjoint(chunk):
        _, first, subs = CHUNKS[chunk]
        each(1, NZ, lambda d: zx_copy(chunk, d, (z - d + NZ) % NZ).wait_recv())
        half = half_of(chunk)
        corr = zx_bufs[chunk][0].astype(jnp.float32)
        for slot in range(1, NZ):
            corr = corr + zx_bufs[chunk][slot].astype(jnp.float32)
        for sub in range(subs):
            value = kept[half, first + sub] * (
                norm_factor * corr[sub] - obs_buf[half, first + sub]
            )
            adj[part_k, half, first + sub, pl.ds(row_k, ROWS), :] = value.astype(
                jnp.bfloat16
            )
        for dy, dx in PLANE_PEERS:
            ag_copy(chunk, dy * NX + dx, k).start()

    def gather(chunk):
        def wait(d):
            from_y = (y - d // NX + NY) % NY
            from_x = (x - d % NX + NX) % NX
            ag_copy(chunk, d, from_y * NX + from_x).wait_recv()

        each(1, PLANE, wait)

    def store(chunk):
        _, first, subs = CHUNKS[chunk]
        half = half_of(chunk)
        return pltpu.make_async_copy(
            adj.at[:, half, pl.ds(first, subs)],
            adjoint_ref.at[:, half, pl.ds(first, subs)],
            local_sem.at[5 + chunk],
        )

    def swap(piece):
        spots = pl.ds(piece * WIDTH, WIDTH)
        return pltpu.make_async_remote_copy(
            src_ref=k_own,
            dst_ref=k_other,
            send_sem=kx_send.at[piece],
            recv_sem=kx_recv.at[piece],
            device_id=(me, other),
            device_id_type=MESH,
        )

    def wave(chunk):
        _, first, subs = CHUNKS[chunk]
        half = half_of(chunk)
        count_rows = subs * SUB
        rows = pl.ds(first * SUB, count_rows)
        res_re = adj[0, half, first : first + subs].reshape(count_rows, HALF)
        res_im = adj[1, half, first : first + subs].reshape(count_rows, HALF)
        residual = jnp.concatenate(
            [
                jnp.concatenate([res_re, -res_im], axis=1),
                jnp.concatenate([res_im, res_re], axis=1),
            ],
            axis=0,
        )
        for piece in range(points // WIDTH):
            spots = pl.ds(piece * WIDTH, WIDTH)
            own = g_all[c, :, :, spots].reshape(2 * HALF, WIDTH)
            product = dot_nn(residual, own)
            real, imag = product[:count_rows], product[count_rows:]
            row_re = g_all[half, 0, rows, spots].astype(jnp.float32)
            row_im = g_all[half, 1, rows, spots].astype(jnp.float32)
            terms = real * row_re + imag * row_im
            terms = jnp.sum(terms.reshape(count_rows // 8, 8, WIDTH), axis=0)
            if chunk > 0:
                terms = terms + k_acc[:, spots]
            if chunk < count - 1:
                k_acc[:, spots] = terms
            else:
                k_own[:, spots] = norm_factor * jnp.sum(terms, axis=0, keepdims=True)

    pl.semaphore_wait(barrier, 1 + len(ring) + len(column) + len(beside) + len(beyond))
    for piece in range(PIECES):
        load(piece).wait()
        exchange(piece).start()
    for pts in (*ring, *beyond):
        pl.semaphore_signal(known, inc=1, device_id=(pts, c), device_id_type=MESH)
    load_source.wait()
    source = source_ref[...]
    weighted[0] = (source * g_all[c, 0].astype(jnp.float32)).astype(jnp.bfloat16)
    weighted[1] = (source * g_all[c, 1].astype(jnp.float32)).astype(jnp.bfloat16)

    correlate(0)

    load_ids.wait()
    load_mask.wait()
    load_obs.wait()
    ids = ids_ref[...].astype(jnp.float32)
    stations = ids.shape[1]
    col_ids = ids_ref[:, pl.ds(pl.multiple_of(c * HALF, HALF), HALF)].astype(jnp.float32)
    spot = lax.broadcasted_iota(jnp.int32, (ROWS, stations), 1)
    row = lax.broadcasted_iota(jnp.int32, (ROWS, stations), 0) + row_k
    for half in range(2):
        for sub in range(2):
            here = spot == row + (half * HALF + sub * SUB)
            row_ids = jnp.sum(jnp.where(here, ids, 0.0), axis=1, keepdims=True)
            keep = (mask_buf[half, sub] == 1) & (row_ids != col_ids)
            kept[half, sub] = jnp.where(keep, 1.0, 0.0)

    pl.semaphore_wait(known, len(ring) + len(beyond))
    scatter(0)
    for chunk in range(1, count):
        correlate(chunk)
        scatter(chunk)
    for chunk in range(count):
        reduce_plane(chunk)
    for piece in range(PIECES):
        exchange(piece).wait_send()
    for chunk in range(count):
        each(1, PLANE, lambda d: rs_copy(chunk, d).wait_send())
    for chunk in range(count):
        make_adjoint(chunk)
    for chunk in range(count):
        each(1, NZ, lambda d: zx_copy(chunk, d, z).wait_send())
    for chunk in range(count):
        if chunk == count - 1:
            for sent in range(count - 1):
                each(1, PLANE, lambda d: ag_copy(sent, d, k).wait_send())
        gather(chunk)
        store(chunk).start()
        wave(chunk)
        if chunk == count - 1:
            swap(0).start()

    each(1, PLANE, lambda d: ag_copy(count - 1, d, k).wait_send())
    for chunk in range(count):
        store(chunk).wait()
    swap(0).wait()
    kernel_ref[...] = k_own[...] + k_other[...]


def body(greens, source, observed, pair_mask, block_ids):
    own_count, points = greens.shape[1], greens.shape[2]
    stations = observed.shape[1]
    norm_factor = float(points * lax.axis_size("pts")) ** (-0.5)
    vmem = pl.BlockSpec(memory_space=pltpu.VMEM)
    hbm = pl.BlockSpec(memory_space=pltpu.HBM)
    anywhere = pl.BlockSpec(memory_space=pl.ANY)
    dma = pltpu.SemaphoreType.DMA
    bf16, f32 = jnp.bfloat16, jnp.float32
    count = len(CHUNKS)
    pieces = points // WIDTH

    def blocks(slots):
        return [pltpu.VMEM((slots, subs, ROWS, HALF), bf16) for _, _, subs in CHUNKS]

    operands = (
        greens,
        source.reshape(1, points),
        observed.reshape(2, 2, 2, SUB, HALF),
        pair_mask.reshape(2, 2, SUB, HALF),
        block_ids.reshape(1, stations),
    )
    kernel, adjoint = pl.pallas_call(
        functools.partial(kernel_body, norm_factor),
        out_shape=(
            jax.ShapeDtypeStruct((1, points), f32),
            jax.ShapeDtypeStruct((2, 2, 2, SUB, HALF), bf16),
        ),
        in_specs=[hbm] * 5,
        out_specs=(vmem, anywhere),
        scratch_shapes=[
            pltpu.VMEM((2, 2, HALF, points), bf16),
            pltpu.VMEM((2, HALF, points), bf16),
            pltpu.VMEM((2, 2, 2, SUB, HALF), bf16),
            pltpu.VMEM((2, 2, ROWS, HALF), f32),
            pltpu.VMEM((2, 2, ROWS, HALF), jnp.int32),
            pltpu.VMEM((2, 2, ROWS, HALF), f32),
            pltpu.VMEM((1, points), f32),
            pltpu.VMEM((1, stations), jnp.int32),
            pltpu.VMEM((8, points), f32),
            pltpu.VMEM((1, points), f32),
            pltpu.VMEM((1, points), f32),
            pltpu.SemaphoreType.REGULAR,
            dma((PIECES,)),
            dma((5 + count,)),
            dma((PIECES,)),
            dma((PIECES,)),
            dma((count, PLANE)),
            dma((count, PLANE)),
            dma((count, NZ)),
            dma((count, NZ)),
            dma((count, PLANE)),
            dma((count, PLANE)),
            dma((pieces,)),
            dma((pieces,)),
            *blocks(PLANE),
            *blocks(PLANE),
            *blocks(NZ),
        ],
        compiler_params=pltpu.CompilerParams(
            collective_id=0, has_side_effects=True, vmem_limit_bytes=48 * 2**20
        ),
        cost_estimate=pl.CostEstimate(
            flops=16 * stations * own_count * points,
            bytes_accessed=8 * 2**20,
            transcendentals=0,
        ),
        name="noise_kernel",
    )(*(pltpu.with_memory_space_constraint(operand, pltpu.HBM) for operand in operands))
    return kernel.reshape(points), adjoint.reshape(2, stations, own_count)


def solution(mesh):
    placed = (P(None, "sta", "pts"), P("pts"), P(None, None, "sta"), P(None, "sta"), P())
    return jax.shard_map(
        body,
        mesh=mesh,
        in_specs=placed,
        out_specs=(P("pts"), P(None, None, "sta")),
        check_vma=False,
    )
```

```python
import functools

import jax
import jax.numpy as jnp
from jax import lax
from jax.experimental import pallas as pl
from jax.experimental.pallas import tpu as pltpu
from jax.sharding import PartitionSpec as P

NY, NZ, NX = 4, 8, 4
PLANE = NY * NX
HALF = 256
SUB = 128
ROWS = 16
GROUPS = SUB // ROWS
WIDTH = 2048
CHUNKS = ((0, 0, 2), (1, 0, 2))
PIECES = 8
MESH = pl.DeviceIdType.MESH
PLANE_PEERS = (
    (2, 2), (3, 2), (2, 3), (1, 2), (2, 1), (0, 2), (2, 0), (3, 1),
    (1, 3), (3, 3), (1, 1), (3, 0), (0, 3), (1, 0), (0, 1),
)
LINE_PEERS = (4, 3, 5, 2, 6, 1, 7)


def dot_nt(left, right):
    return lax.dot_general(
        left, right, (((1,), (1,)), ((), ())), preferred_element_type=jnp.float32
    )


def dot_nn(left, right):
    return lax.dot_general(
        left, right, (((1,), (0,)), ((), ())), preferred_element_type=jnp.float32
    )


def kernel_body(
    norm_factor,
    greens_ref,
    source_hbm,
    observed_ref,
    mask_ref,
    ids_hbm,
    kernel_ref,
    adjoint_ref,
    g_all,
    weighted,
    adj,
    obs_buf,
    mask_buf,
    kept,
    source_ref,
    ids_ref,
    k_acc,
    k_own,
    k_other,
    known,
    load_sem,
    local_sem,
    gx_send,
    gx_recv,
    rs_send,
    rs_recv,
    zx_send,
    zx_recv,
    ag_send,
    ag_recv,
    kx_send,
    kx_recv,
    *buffers,
):
    count = len(CHUNKS)
    part_bufs = buffers[:count]
    rs_bufs = buffers[count : 2 * count]
    zx_bufs = buffers[2 * count :]
    points = greens_ref.shape[2]
    me = lax.axis_index("pts")
    c = lax.axis_index("sta")
    other = 1 - c
    x = me % NX
    z = (me // NX) % NZ
    y = me // (NX * NZ)
    k = y * NX + x
    part_k = k // GROUPS
    row_k = pl.multiple_of((k % GROUPS) * ROWS, ROWS)

    def plane_peer(d):
        py = (y + d // NX) % NY
        px = (x + d % NX) % NX
        return py * NX + px, (py * NZ + z) * NX + px

    def line_peer(d):
        pz = (z + d) % NZ
        return pz, (y * NZ + pz) * NX + x

    def each(start, stop, step):
        def once(d, carry):
            step(d)
            return carry

        lax.fori_loop(start, stop, once, 0)

    barrier = pltpu.get_barrier_semaphore()
    ring = [plane_peer(d)[1] for d in range(1, NX)]
    column = [plane_peer(d * NX)[1] for d in range(1, NY)]
    beside = [line_peer(d)[1] for d in (1, NZ - 1)]
    beyond = [line_peer(d)[1] for d in (2, NZ - 2)]
    pl.semaphore_signal(barrier, inc=1, device_id=(me, other), device_id_type=MESH)
    for pts in (*ring, *column, *beyond, *beside):
        pl.semaphore_signal(barrier, inc=1, device_id=(pts, c), device_id_type=MESH)

    def load(piece):
        span = points // PIECES
        spots = pl.ds(piece * span, span)
        return pltpu.make_async_copy(
            greens_ref.at[:, :, spots], g_all.at[c, :, :, spots], load_sem.at[piece]
        )

    for piece in range(PIECES):
        load(piece).start()
    load_source = pltpu.make_async_copy(source_hbm, source_ref, local_sem.at[1])
    load_source.start()

    def exchange(piece):
        span = points // PIECES
        spots = pl.ds(piece * span, span)
        return pltpu.make_async_remote_copy(
            src_ref=g_all.at[c, :, :, spots],
            dst_ref=g_all.at[c, :, :, spots],
            send_sem=gx_send.at[piece],
            recv_sem=gx_recv.at[piece],
            device_id=(me, other),
            device_id_type=MESH,
        )

    load_ids = pltpu.make_async_copy(ids_hbm, ids_ref, local_sem.at[2])
    load_ids.start()
    load_obs = pltpu.make_async_copy(
        observed_ref.at[part_k, :, :, pl.ds(row_k, ROWS), :], obs_buf, local_sem.at[3]
    )
    load_obs.start()
    load_mask = pltpu.make_async_copy(
        mask_ref.at[:, :, pl.ds(row_k, ROWS), :], mask_buf, local_sem.at[4]
    )
    load_mask.start()

    def rs_copy(chunk, d):
        peer, peer_pts = plane_peer(d)
        return pltpu.make_async_remote_copy(
            src_ref=part_bufs[chunk].at[peer],
            dst_ref=rs_bufs[chunk].at[d],
            send_sem=rs_send.at[chunk, d],
            recv_sem=rs_recv.at[chunk, d],
            device_id=(peer_pts, c),
            device_id_type=MESH,
        )

    def zx_copy(chunk, d, slot):
        return pltpu.make_async_remote_copy(
            src_ref=zx_bufs[chunk].at[slot],
            dst_ref=zx_bufs[chunk].at[slot],
            send_sem=zx_send.at[chunk, d],
            recv_sem=zx_recv.at[chunk, d],
            device_id=(line_peer(d)[1], c),
            device_id_type=MESH,
        )

    def half_of(chunk):
        return (c + CHUNKS[chunk][0]) % 2

    def ag_copy(chunk, d, owner):
        _, first, subs = CHUNKS[chunk]
        rows = pl.multiple_of((owner % GROUPS) * ROWS, ROWS)
        block = adj.at[
            owner // GROUPS, half_of(chunk), pl.ds(first, subs), pl.ds(rows, ROWS), :
        ]
        return pltpu.make_async_remote_copy(
            src_ref=block,
            dst_ref=block,
            send_sem=ag_send.at[chunk, d],
            recv_sem=ag_recv.at[chunk, d],
            device_id=(plane_peer(d)[1], c),
            device_id_type=MESH,
        )

    def correlate(chunk):
        half = half_of(chunk)
        real = jnp.zeros((HALF, HALF), jnp.float32)
        imag = jnp.zeros((HALF, HALF), jnp.float32)
        span = points // PIECES
        for piece in range(PIECES):
            if chunk > 0:
                exchange(piece).wait_recv()
            spots = pl.ds(piece * span, span)
            rows_re = g_all[half, 0, :, spots]
            rows_im = g_all[half, 1, :, spots]
            own_re = weighted[0, :, spots]
            own_im = weighted[1, :, spots]
            real += dot_nt(rows_re, own_re) + dot_nt(rows_im, own_im)
            imag += dot_nt(rows_im, own_re) - dot_nt(rows_re, own_im)
        for part, value in enumerate((real, imag)):
            for sub in range(2):
                block = value[sub * SUB : (sub + 1) * SUB].astype(jnp.bfloat16)
                part_bufs[chunk][part * GROUPS : (part + 1) * GROUPS, sub] = block.reshape(
                    GROUPS, ROWS, HALF
                )

    def scatter(chunk, peers=PLANE_PEERS):
        for dy, dx in peers:
            rs_copy(chunk, dy * NX + dx).start()

    def reduce_plane(chunk):
        def add(d, total):
            rs_copy(chunk, d).wait_recv()
            return total + rs_bufs[chunk][d].astype(jnp.float32)

        total = lax.fori_loop(1, PLANE, add, part_bufs[chunk][k].astype(jnp.float32))
        zx_bufs[chunk][z] = total.astype(jnp.bfloat16)
        for d in LINE_PEERS:
            zx_copy(chunk, d, z).start()

    def make_adjoint(chunk):
        _, first, subs = CHUNKS[chunk]
        each(1, NZ, lambda d: zx_copy(chunk, d, (z - d + NZ) % NZ).wait_recv())
        half = half_of(chunk)
        corr = zx_bufs[chunk][0].astype(jnp.float32)
        for slot in range(1, NZ):
            corr = corr + zx_bufs[chunk][slot].astype(jnp.float32)
        for sub in range(subs):
            value = kept[half, first + sub] * (
                norm_factor * corr[sub] - obs_buf[half, first + sub]
            )
            adj[part_k, half, first + sub, pl.ds(row_k, ROWS), :] = value.astype(
                jnp.bfloat16
            )
        for dy, dx in PLANE_PEERS:
            ag_copy(chunk, dy * NX + dx, k).start()

    def gather(chunk):
        def wait(d):
            from_y = (y - d // NX + NY) % NY
            from_x = (x - d % NX + NX) % NX
            ag_copy(chunk, d, from_y * NX + from_x).wait_recv()

        each(1, PLANE, wait)

    def store(chunk):
        _, first, subs = CHUNKS[chunk]
        half = half_of(chunk)
        return pltpu.make_async_copy(
            adj.at[:, half, pl.ds(first, subs)],
            adjoint_ref.at[:, half, pl.ds(first, subs)],
            local_sem.at[5 + chunk],
        )

    def swap(piece):
        spots = pl.ds(piece * WIDTH, WIDTH)
        return pltpu.make_async_remote_copy(
            src_ref=k_own.at[:, spots],
            dst_ref=k_other.at[:, spots],
            send_sem=kx_send.at[piece],
            recv_sem=kx_recv.at[piece],
            device_id=(me, other),
            device_id_type=MESH,
        )

    def wave(chunk):
        _, first, subs = CHUNKS[chunk]
        half = half_of(chunk)
        count_rows = subs * SUB
        rows = pl.ds(first * SUB, count_rows)
        res_re = adj[0, half, first : first + subs].reshape(count_rows, HALF)
        res_im = adj[1, half, first : first + subs].reshape(count_rows, HALF)
        residual = jnp.concatenate(
            [
                jnp.concatenate([res_re, -res_im], axis=1),
                jnp.concatenate([res_im, res_re], axis=1),
            ],
            axis=0,
        )
        for piece in range(points // WIDTH):
            spots = pl.ds(piece * WIDTH, WIDTH)
            own = g_all[c, :, :, spots].reshape(2 * HALF, WIDTH)
            product = dot_nn(residual, own)
            real, imag = product[:count_rows], product[count_rows:]
            row_re = g_all[half, 0, rows, spots].astype(jnp.float32)
            row_im = g_all[half, 1, rows, spots].astype(jnp.float32)
            terms = real * row_re + imag * row_im
            terms = jnp.sum(terms.reshape(count_rows // 8, 8, WIDTH), axis=0)
            if chunk > 0:
                terms = terms + k_acc[:, spots]
            if chunk < count - 1:
                k_acc[:, spots] = terms
            else:
                k_own[:, spots] = norm_factor * jnp.sum(terms, axis=0, keepdims=True)
                swap(piece).start()

    pl.semaphore_wait(barrier, 1 + len(ring) + len(column) + len(beside) + len(beyond))
    for piece in range(PIECES):
        load(piece).wait()
        exchange(piece).start()
    for pts in (*ring, *beyond):
        pl.semaphore_signal(known, inc=1, device_id=(pts, c), device_id_type=MESH)
    load_source.wait()
    source = source_ref[...]
    weighted[0] = (source * g_all[c, 0].astype(jnp.float32)).astype(jnp.bfloat16)
    weighted[1] = (source * g_all[c, 1].astype(jnp.float32)).astype(jnp.bfloat16)

    correlate(0)

    load_ids.wait()
    load_mask.wait()
    load_obs.wait()
    ids = ids_ref[...].astype(jnp.float32)
    stations = ids.shape[1]
    col_ids = ids_ref[:, pl.ds(pl.multiple_of(c * HALF, HALF), HALF)].astype(jnp.float32)
    spot = lax.broadcasted_iota(jnp.int32, (ROWS, stations), 1)
    row = lax.broadcasted_iota(jnp.int32, (ROWS, stations), 0) + row_k
    for half in range(2):
        for sub in range(2):
            here = spot == row + (half * HALF + sub * SUB)
            row_ids = jnp.sum(jnp.where(here, ids, 0.0), axis=1, keepdims=True)
            keep = (mask_buf[half, sub] == 1) & (row_ids != col_ids)
            kept[half, sub] = jnp.where(keep, 1.0, 0.0)

    pl.semaphore_wait(known, len(ring) + len(beyond))
    scatter(0)
    for chunk in range(1, count):
        correlate(chunk)
        scatter(chunk)
    for chunk in range(count):
        reduce_plane(chunk)
    for chunk in range(count):
        make_adjoint(chunk)
    for piece in range(PIECES):
        exchange(piece).wait_send()
    for chunk in range(count):
        each(1, PLANE, lambda d: rs_copy(chunk, d).wait_send())
    for chunk in range(count):
        each(1, NZ, lambda d: zx_copy(chunk, d, z).wait_send())
    for chunk in range(count):
        if chunk == count - 1:
            for sent in range(count - 1):
                each(1, PLANE, lambda d: ag_copy(sent, d, k).wait_send())
        gather(chunk)
        store(chunk).start()
        wave(chunk)

    each(1, PLANE, lambda d: ag_copy(count - 1, d, k).wait_send())
    for chunk in range(count):
        store(chunk).wait()
    for piece in range(points // WIDTH):
        swap(piece).wait()
    kernel_ref[...] = k_own[...] + k_other[...]


def body(greens, source, observed, pair_mask, block_ids):
    own_count, points = greens.shape[1], greens.shape[2]
    stations = observed.shape[1]
    norm_factor = float(points * lax.axis_size("pts")) ** (-0.5)
    vmem = pl.BlockSpec(memory_space=pltpu.VMEM)
    hbm = pl.BlockSpec(memory_space=pltpu.HBM)
    anywhere = pl.BlockSpec(memory_space=pl.ANY)
    dma = pltpu.SemaphoreType.DMA
    bf16, f32 = jnp.bfloat16, jnp.float32
    count = len(CHUNKS)
    pieces = points // WIDTH

    def blocks(slots):
        return [pltpu.VMEM((slots, subs, ROWS, HALF), bf16) for _, _, subs in CHUNKS]

    operands = (
        greens,
        source.reshape(1, points),
        observed.reshape(2, 2, 2, SUB, HALF),
        pair_mask.reshape(2, 2, SUB, HALF),
        block_ids.reshape(1, stations),
    )
    kernel, adjoint = pl.pallas_call(
        functools.partial(kernel_body, norm_factor),
        out_shape=(
            jax.ShapeDtypeStruct((1, points), f32),
            jax.ShapeDtypeStruct((2, 2, 2, SUB, HALF), bf16),
        ),
        in_specs=[hbm] * 5,
        out_specs=(vmem, anywhere),
        scratch_shapes=[
            pltpu.VMEM((2, 2, HALF, points), bf16),
            pltpu.VMEM((2, HALF, points), bf16),
            pltpu.VMEM((2, 2, 2, SUB, HALF), bf16),
            pltpu.VMEM((2, 2, ROWS, HALF), f32),
            pltpu.VMEM((2, 2, ROWS, HALF), jnp.int32),
            pltpu.VMEM((2, 2, ROWS, HALF), f32),
            pltpu.VMEM((1, points), f32),
            pltpu.VMEM((1, stations), jnp.int32),
            pltpu.VMEM((8, points), f32),
            pltpu.VMEM((1, points), f32),
            pltpu.VMEM((1, points), f32),
            pltpu.SemaphoreType.REGULAR,
            dma((PIECES,)),
            dma((5 + count,)),
            dma((PIECES,)),
            dma((PIECES,)),
            dma((count, PLANE)),
            dma((count, PLANE)),
            dma((count, NZ)),
            dma((count, NZ)),
            dma((count, PLANE)),
            dma((count, PLANE)),
            dma((pieces,)),
            dma((pieces,)),
            *blocks(PLANE),
            *blocks(PLANE),
            *blocks(NZ),
        ],
        compiler_params=pltpu.CompilerParams(
            collective_id=0, has_side_effects=True, vmem_limit_bytes=48 * 2**20
        ),
        cost_estimate=pl.CostEstimate(
            flops=16 * stations * own_count * points,
            bytes_accessed=8 * 2**20,
            transcendentals=0,
        ),
        name="noise_kernel",
    )(*(pltpu.with_memory_space_constraint(operand, pltpu.HBM) for operand in operands))
    return kernel.reshape(points), adjoint.reshape(2, stations, own_count)


def solution(mesh):
    placed = (P(None, "sta", "pts"), P("pts"), P(None, None, "sta"), P(None, "sta"), P())
    return jax.shard_map(
        body,
        mesh=mesh,
        in_specs=placed,
        out_specs=(P("pts"), P(None, None, "sta")),
        check_vma=False,
    )
```
